512 devices in a mesh: fsdp: 64 (over y_lo, z, x), tp: 8 (over y_hi, core).
Axes of the slice: x: 4, y: 8 (y_hi: 4, y_lo: 2; y = y_hi * 2 + y_lo), z: 8, core: 2. Of those that a mesh axis runs over, the one named last changes fastest.
Arguments:
- hidden: bfloat16 [4096, 5120], P('fsdp', 'tp'), may hold values from -6 to 6
- next_hidden: bfloat16 [4096, 5120], P('fsdp', 'tp'), may hold values from -6 to 6
- gain: bfloat16 [5120], replicated, may hold values from 0.5 to 2
- w_query: bfloat16 [5120, 4096], P('fsdp', 'tp'), may hold values from -0.078125 to 0.078125
- w_key: bfloat16 [5120, 1024], P('fsdp', 'tp'), may hold values from -0.078125 to 0.078125
- w_value: bfloat16 [5120, 1024], P('fsdp', 'tp'), may hold values from -0.078125 to 0.078125
- w_out: bfloat16 [4096, 5120], P('tp', 'fsdp'), may hold values from -0.09375 to 0.09375
- key_cache: bfloat16 [4096, 8, 128, 128], P('fsdp', 'tp'), may hold values from -400 to 400
- value_cache: bfloat16 [4096, 8, 128, 128], P('fsdp', 'tp'), may hold values from -6 to 6
- lengths: int32 [4096], P('fsdp'), may hold values from 1 to 128, as said below
- positions: int32 [4096], P('fsdp'), may hold values from 1 to 8319, as said below
Outputs:
- layer_out: bfloat16 [64, 2, 64, 5120], P(None, None, 'fsdp', 'tp')
The draws below stay inside these ranges and needn't reach their ends.
Inputs may be any that keep to these rules, and one draw needn't show every extreme that they name: `lengths`: the first sequence of every rollout group has all 128 slots live, the second exactly one. positions[r] >= lengths[r]; the new tokens of sequence r stand at positions[r] and positions[r] + 1.
All inputs are finite; a program needn't handle non-finite values.
Results may differ from the reference program's by a relative error of at most 0.012.
Values may be sent and summed in bfloat16 or wider, within the bound.
A program may use at most 128 MiB of HBM per device.

```python
import math
import jax
import jax.numpy as jnp
from jax import lax

D = 5120
QH = 32
KVH = 8
HD = 128
ROWS = 64
CACHE = 128
ALL_ROWS = 4096
N_FSDP = 64


def cache_fill(key):
    filled = jax.random.randint(key, (ALL_ROWS,), 1, CACHE + 1, dtype=jnp.int32)
    slot = jnp.arange(ALL_ROWS, dtype=jnp.int32) % ROWS
    filled = jnp.where(slot == 0, CACHE, filled)
    return jnp.where(slot == 1, 1, filled)


def draw_lengths(key, part):
    return cache_fill(key)


def draw_positions(key, part):
    filled = cache_fill(key)
    key = jax.random.fold_in(key, 5)
    offsets = jax.random.randint(key, (ALL_ROWS,), 0, 8192, dtype=jnp.int32)
    slot = jnp.arange(ALL_ROWS, dtype=jnp.int32) % ROWS
    offsets = jnp.where(slot == 0, 8191, offsets)
    offsets = jnp.where(slot == 1, 0, offsets)
    return filled + offsets


def draw_key_cache(key, part):
    key = jax.random.fold_in(key, 11)
    base = jnp.clip(jax.random.normal(key, (ALL_ROWS, KVH, CACHE, HD), jnp.float32), -6.0, 6.0)
    return base.astype(jnp.bfloat16)


def steps_of(rng, extent, cuts, smallest, high):
    loudness, own = 1.0, jax.random.fold_in(rng, 6)
    for position, shards_of in cuts:
        draws = jnp.exp(jax.random.uniform(jax.random.fold_in(own, position), (shards_of,), jnp.float32, smallest / len(cuts), high / len(cuts)))
        loudness = loudness * jnp.repeat(draws, extent[position] // shards_of).reshape([-1 if axis == position else 1 for axis in range(len(extent))])
    return loudness


def scatter_about(rng, extent, deviation, most, shards=(), held_as=jnp.bfloat16):
    drawn = jax.random.normal(rng, extent, jnp.float32) * deviation
    if len(shards) > 0:
        drawn = steps_of(rng, extent, shards, -0.22, 0.18) * drawn
    return jnp.clip(drawn, min=-most, max=most).astype(held_as)


def setup_inputs(seed: int = 0) -> dict:
    key_list = jax.random.split(jax.random.key(seed), 12)
    return {
        "hidden": scatter_about(key_list[0], (ALL_ROWS, D), 1.0, 6.0, ((0, 64), (1, 8))),
        "next_hidden": scatter_about(key_list[1], (ALL_ROWS, D), 1.0, 6.0, ((0, 64), (1, 8))),
        "gain": jnp.clip(jnp.exp(jax.random.uniform(key_list[2], (D,), jnp.float32, math.log(0.5), math.log(2.0))), 0.5, 2.0).astype(jnp.bfloat16),
        "w_query": scatter_about(key_list[3], (D, QH * HD), D ** -0.5, 0.078125, ((0, 64), (1, 8))),
        "w_key": scatter_about(key_list[4], (D, KVH * HD), D ** -0.5, 0.078125, ((0, 64), (1, 8))),
        "w_value": scatter_about(key_list[5], (D, KVH * HD), D ** -0.5, 0.078125, ((0, 64), (1, 8))),
        "w_out": scatter_about(key_list[6], (QH * HD, D), (QH * HD) ** -0.5, 0.09375, ((0, 8), (1, 64))),
        "key_cache": draw_key_cache(jax.random.fold_in(key_list[11], 71), 0),
        "value_cache": scatter_about(key_list[8], (ALL_ROWS, KVH, CACHE, HD), 1.0, 6.0, ((0, 64), (1, 8))),
        "lengths": draw_lengths(jax.random.fold_in(key_list[11], 71), 0),
        "positions": draw_positions(jax.random.fold_in(key_list[11], 71), 0),
    }


RMS_EPS = 1e-06
ROPE_BASE = 1000000.0

def normalize(rows_in, gain):
    values = rows_in.astype(jnp.float32)
    square = lax.optimization_barrier(jnp.mean(values * values, axis=-1, keepdims=True))
    return (values * lax.rsqrt(square + RMS_EPS) * gain.astype(jnp.float32)).astype(jnp.bfloat16)

def rotate(vectors, where_at):
    half = vectors.shape[-1] // 2
    freqs = ROPE_BASE ** (-(2.0 * jnp.arange(half, dtype=jnp.float32)) / vectors.shape[-1])
    angle = where_at.astype(jnp.float32)[:, :, None, None] * freqs
    cosine = jnp.cos(angle)
    sine = jnp.sin(angle)
    first = vectors[..., :half]
    second = vectors[..., half:]
    return jnp.concatenate([first * cosine - second * sine, second * cosine + first * sine], axis=-1)

def attend_group(queries, keys_new, values_new, key_cache, value_cache, lengths):
    score_scale = queries.shape[-1] ** (-0.5)
    query_wide = queries.astype(jnp.float32)
    cache_scores = jnp.einsum('srkgd,rkcd->srkgc', query_wide, key_cache.astype(jnp.float32)) * score_scale
    live = jnp.arange(key_cache.shape[2], dtype=jnp.int32)[None, :] < lengths[:, None]
    cache_scores = jnp.where(live[None, :, None, None, :], cache_scores, -jnp.inf)
    new_scores = jnp.einsum('srkgd,trkd->srkgt', query_wide, keys_new.astype(jnp.float32)) * score_scale
    causal = jnp.arange(2, dtype=jnp.int32)[:, None] >= jnp.arange(2, dtype=jnp.int32)[None, :]
    new_scores = jnp.where(causal[:, None, None, None, :], new_scores, -jnp.inf)
    row_top = jnp.maximum(lax.optimization_barrier(jnp.max(cache_scores, axis=-1)), lax.optimization_barrier(jnp.max(new_scores, axis=-1)))[..., None]
    cache_probs = jnp.exp(cache_scores - row_top)
    new_probs = jnp.exp(new_scores - row_top)
    total = lax.optimization_barrier(jnp.sum(cache_probs, axis=-1)) + lax.optimization_barrier(jnp.sum(new_probs, axis=-1))
    cache_weights = cache_probs.astype(jnp.bfloat16).astype(jnp.float32)
    new_weights = new_probs.astype(jnp.bfloat16).astype(jnp.float32)
    mixed = jnp.einsum('srkgc,rkcd->srkgd', cache_weights, value_cache.astype(jnp.float32))
    mixed = mixed + jnp.einsum('srkgt,trkd->srkgd', new_weights, values_new.astype(jnp.float32))
    return (mixed / total[..., None]).astype(jnp.bfloat16)

def reference(hidden, next_hidden, gain, w_query, w_key, w_value, w_out, key_cache, value_cache, lengths, positions):
    both = jnp.stack([hidden, next_hidden])
    normed = normalize(both, gain).reshape(2 * ALL_ROWS, D)
    queries = jnp.dot(normed, w_query, preferred_element_type=jnp.float32).reshape(2, ALL_ROWS, QH, HD)
    keys_new = jnp.dot(normed, w_key, preferred_element_type=jnp.float32).reshape(2, ALL_ROWS, KVH, HD)
    values_new = jnp.dot(normed, w_value, preferred_element_type=jnp.float32).reshape(2, ALL_ROWS, KVH, HD)
    where_at = positions[None, :] + jnp.arange(2, dtype=jnp.int32)[:, None]
    queries = rotate(queries, where_at).astype(jnp.bfloat16)
    keys_new = rotate(keys_new, where_at).astype(jnp.bfloat16)
    values_new = values_new.astype(jnp.bfloat16)
    group_queries = queries.reshape(2, N_FSDP, ROWS, KVH, QH // KVH, HD).transpose(1, 0, 2, 3, 4, 5)
    group_keys = keys_new.reshape(2, N_FSDP, ROWS, KVH, HD).transpose(1, 0, 2, 3, 4)
    group_values = values_new.reshape(2, N_FSDP, ROWS, KVH, HD).transpose(1, 0, 2, 3, 4)
    group_key_cache = key_cache.reshape(N_FSDP, ROWS, KVH, CACHE, HD)
    group_value_cache = value_cache.reshape(N_FSDP, ROWS, KVH, CACHE, HD)
    group_lengths = lengths.reshape(N_FSDP, ROWS)

    def one_group(items):
        return attend_group(items[0], items[1], items[2], items[3], items[4], items[5])
    attended = lax.map(one_group, (group_queries, group_keys, group_values, group_key_cache, group_value_cache, group_lengths))
    attended = attended.reshape(N_FSDP * 2 * ROWS, QH * HD)
    projected = jnp.dot(attended, w_out, preferred_element_type=jnp.float32).reshape(N_FSDP, 2, ROWS, D)
    residual = both.reshape(2, N_FSDP, ROWS, D).transpose(1, 0, 2, 3).astype(jnp.float32)
    return (residual + projected).astype(jnp.bfloat16)
```

```python
import functools

import jax
import jax.numpy as jnp
from jax import lax
from jax.experimental import pallas as pl
from jax.experimental.pallas import tpu as pltpu
from jax.sharding import PartitionSpec as P

RMS_EPS = 1e-06
ROPE_BASE = 1000000.0
MESH = pl.DeviceIdType.MESH
NX, NZ, NYH = 4, 8, 4
CHUNK = 16

f32, bf16 = jnp.float32, jnp.bfloat16


def one_hot_rows(out_dims, source_of):
    count = 1
    for size in out_dims:
        count *= size
    row = lax.broadcasted_iota(jnp.int32, (count, count), 0)
    column = lax.broadcasted_iota(jnp.int32, (count, count), 1)
    digits, shift = [], 0
    for size in reversed(out_dims):
        bits = size.bit_length() - 1
        digits.append(lax.shift_right_logical(row, shift) & (size - 1))
        shift += bits
    digits.reverse()
    return jnp.where(source_of(*digits) == column, 1.0, 0.0).astype(bf16)


def pick(matrix, rows):
    return jnp.dot(matrix, rows, preferred_element_type=f32)


def layer_kernel(
    hid, nxt, gain, wq, wk, wv, wot, cos_ref, sin_ref, live_ref, kc_hbm, vc_hbm,
    out,
    wa, wb, oa, ob, xs, xg, xn, ssb, ssr, qs, qr, kc, vc, q3, att3, attb,
    ps, pr, pk, sp, rb, rr, zs, zr, xo, xr,
    cache_sem, xs_send, xs_recv, sib_send, sib_recv, res_send, res_recv,
    ax_send, ax_recv, az_send, az_recv, bx_send, bx_recv, bz_send, bz_recv,
    pair_send, pair_recv, core_send, core_recv, y_send, y_recv,
    za_send, za_recv, xa_send, xa_recv,
):
    rows = hid.shape[0]
    half = rows // 2
    both = 2 * rows
    width = hid.shape[1]
    block = wq.shape[0]
    tile_blocks = NYH
    f, t = lax.axis_index("fsdp"), lax.axis_index("tp")
    x, z, yl = lax.rem(f, NX), lax.rem(f // NX, NZ), f // (NX * NZ)
    yh, c = t // 2, lax.rem(t, 2)

    def dev(x_, z_, yl_, yh_, c_):
        return ((yl_ * NZ + z_) * NX + x_, yh_ * 2 + c_)

    def remote(src, dst, send, recv, where):
        return pltpu.make_async_remote_copy(
            src_ref=src, dst_ref=dst, send_sem=send, recv_sem=recv,
            device_id=where, device_id_type=MESH,
        )

    def arrived(dst, sem):
        pltpu.make_async_copy(dst, dst, sem).wait()

    sent = []

    def send(*args):
        copy = remote(*args)
        copy.start()
        sent.append(copy)

    key_load = pltpu.make_async_copy(kc_hbm, kc, cache_sem.at[0])
    value_load = pltpu.make_async_copy(vc_hbm, vc, cache_sem.at[1])
    key_load.start()
    value_load.start()

    y = 2 * yh + yl
    ny = 2 * NYH
    sib = dev(x, z, yl, yh, 1 - c)
    partner = dev(x, z, 1 - yl, yh, c)
    places = [dev(lax.rem(x + d, NX), z, yl, yh, c) for d in range(1, NX)]
    places += [dev(x, lax.rem(z + d, NZ), yl, yh, c) for d in range(1, NZ)]
    for d in range(1, ny):
        yy = lax.rem(y + d, ny)
        places.append(dev(x, z, lax.rem(yy, 2), yy // 2, c))
    places.append(sib)
    barrier = pltpu.get_barrier_semaphore()
    for where in places:
        pl.semaphore_signal(barrier, inc=1, device_id=where, device_id_type=MESH)

    mine = pl.ds(pl.multiple_of(x * block, block), block)
    cut = wa.shape[2]
    own = jnp.concatenate([wq[...], wk[...], wv[...]], axis=1)
    wa[z, mine, :] = own[:, :cut]
    wb[z, mine, :] = own[:, cut:]
    ocut = oa.shape[2]
    oa[z, mine, :] = wot[:, :ocut]
    ob[z, mine, :] = wot[:, ocut:]
    xs[0:rows, :] = hid[...]
    xs[rows:both, :] = nxt[...]
    pl.semaphore_wait(barrier, len(places))

    yl_to = yh // (NYH // 2)
    tile_me = lax.rem(yh, NYH // 2) * 2 + c
    src_me = yl * (NYH // 2) + lax.rem(yh, NYH // 2)
    for k in range(NYH):
        is_self = jnp.logical_and(yl_to == yl, yh == k)
        there = dev(x, z, yl_to, k, c)
        away = remote(xs, xg.at[yl, tile_me], xs_send.at[k], xs_recv.at[src_me], there)
        here = pltpu.make_async_copy(xs, xg.at[yl, tile_me], xs_recv.at[src_me])
        pl.when(jnp.logical_not(is_self))(away.start)
        pl.when(is_self)(here.start)

    up = dev(x, lax.rem(z + 1, NZ), yl, yh, c)
    down = dev(x, lax.rem(z + NZ - 1, NZ), yl, yh, c)
    last = NZ // 2 - 1

    def first_x(buf, s):
        for d in range(1, NX):
            there = dev(lax.rem(x + d, NX), z, yl, yh, c)
            send(buf.at[z, mine], buf.at[z, mine], ax_send.at[s, d - 1], ax_recv.at[s, d - 1], there)

    def wait_first_x(buf, s):
        for d in range(1, NX):
            xx = lax.rem(x + NX - d, NX)
            arrived(buf.at[z, pl.ds(pl.multiple_of(xx * block, block), block)], ax_recv.at[s, d - 1])

    def slab_parts(k):
        if k == last:
            h = NX * block // 2
            return pl.ds(0, h), pl.ds(h, h)
        return pl.ds(0, NX * block), pl.ds(0, NX * block)

    def a_send(buf, s, k):
        p_up, p_down = slab_parts(k)
        zz = lax.rem(z + NZ - k, NZ)
        send(buf.at[zz, p_up], buf.at[zz, p_up], az_send.at[s, 0, k], az_recv.at[s, 0, k], up)
        zz = lax.rem(z + k, NZ)
        send(buf.at[zz, p_down], buf.at[zz, p_down], az_send.at[s, 1, k], az_recv.at[s, 1, k], down)

    def a_wait(buf, s, k):
        p_up, p_down = slab_parts(k)
        arrived(buf.at[lax.rem(z + NZ - 1 - k, NZ), p_up], az_recv.at[s, 0, k])
        arrived(buf.at[lax.rem(z + 1 + k, NZ), p_down], az_recv.at[s, 1, k])

    def b_send(buf, s, k):
        zz = lax.rem(z + NZ - k, NZ)
        send(buf.at[zz, mine], buf.at[zz, mine], bz_send.at[s, 0, k], bz_recv.at[s, 0, k], up)
        if k < last:
            zz = lax.rem(z + k, NZ)
            send(buf.at[zz, mine], buf.at[zz, mine], bz_send.at[s, 1, k], bz_recv.at[s, 1, k], down)

    def b_wait(buf, s, k):
        arrived(buf.at[lax.rem(z + NZ - 1 - k, NZ), mine], bz_recv.at[s, 0, k])
        if k < last:
            arrived(buf.at[lax.rem(z + 1 + k, NZ), mine], bz_recv.at[s, 1, k])

    def b_spread(buf, s, offsets):
        for o in offsets:
            zz = lax.rem(z + NZ + o, NZ)
            for d in range(1, NX):
                there = dev(lax.rem(x + d, NX), z, yl, yh, c)
                remote(buf.at[zz, mine], buf.at[zz, mine],
                       bx_send.at[s, d - 1], bx_recv.at[s, d - 1], there).start()

    def spread_after(k):
        return (-1 - k,) if k == last else (-1 - k, 1 + k)

    def wait_spread(buf, s):
        for d in range(1, NX):
            xx = lax.rem(x + NX - d, NX)
            arrived(buf.at[:, pl.ds(pl.multiple_of(xx * block, block), block)], bx_recv.at[s, d - 1])

    first_x(wa, 0)
    b_send(wb, 0, 0)
    b_spread(wb, 0, (0,))

    away_rows = half * (1 - yl)
    own_rows = half * yl
    for s in range(2):
        src = xs.at[pl.ds(pl.multiple_of(s * rows + away_rows, half), half)]
        send(src, rr.at[yl, pl.ds(s * half, half)], res_send.at[s], res_recv.at[s], partner)
        rr[yl, s * half:(s + 1) * half, :] = xs[pl.ds(pl.multiple_of(s * rows + own_rows, half), half), :]

    wait_first_x(wa, 0)
    a_send(wa, 0, 0)
    first_x(oa, 1)
    b_send(ob, 1, 0)
    for k in range(last):
        b_wait(wb, 0, k)
        b_send(wb, 0, k + 1)
        b_spread(wb, 0, spread_after(k))
        a_wait(wa, 0, k)
        a_send(wa, 0, k + 1)

    for k in range(NYH):
        slot = xg.at[k // (NYH // 2), (k % (NYH // 2)) * 2 + c]
        arrived(slot, xs_recv.at[k])
        send(slot, slot, sib_send.at[k], sib_recv.at[k], sib)
    b_wait(wb, 0, last)
    b_spread(wb, 0, spread_after(last))
    for k in range(NYH):
        arrived(xg.at[k // (NYH // 2), (k % (NYH // 2)) * 2 + (1 - c)], sib_recv.at[k])

    for g in range(2):
        total = jnp.zeros((both, 1), f32)
        for j in range(tile_blocks):
            values = xg[g, j].astype(f32)
            total = total + jnp.sum(values * values, axis=1, keepdims=True)
            xn[g, :, j * width:(j + 1) * width] = (values * gain[yl * tile_blocks + j]).astype(bf16)
        ssb[g] = jnp.broadcast_to(total, (both, 128))
    send(ssb.at[1 - yl], ssr, pair_send.at[0], pair_recv.at[0], partner)

    for s in range(2):
        arrived(rr.at[1 - yl, pl.ds(s * half, half)], res_recv.at[s])
    order = one_hot_rows((NZ, 2, NX), lambda z_, s_, x_: s_ * half + z_ * NX + x_)
    for g in range(2):
        rr[g] = pick(order, rr[g]).astype(bf16)

    a_wait(wa, 0, last)
    wait_spread(wb, 0)
    wait_first_x(oa, 1)
    a_send(oa, 1, 0)
    b_spread(ob, 1, (0,))
    b_wait(ob, 1, 0)
    b_send(ob, 1, 1)
    b_spread(ob, 1, spread_after(0))
    depth = NZ * NX * block
    weight_a = wa[...].reshape(depth, cut)
    weight_b = wb[...].reshape(depth, wb.shape[2])
    theirs = xn[1 - yl]
    qs[:, :cut] = jnp.dot(theirs, weight_a, preferred_element_type=f32).astype(bf16)
    qs[:, cut:] = jnp.dot(theirs, weight_b, preferred_element_type=f32).astype(bf16)
    send(qs, qr, pair_send.at[1], pair_recv.at[1], partner)
    ours = xn[yl]
    got_a = jnp.dot(ours, weight_a, preferred_element_type=f32)
    got_b = jnp.dot(ours, weight_b, preferred_element_type=f32)
    got = jnp.concatenate([got_a, got_b], axis=1)

    def out_step(k):
        a_wait(oa, 1, k)
        a_send(oa, 1, k + 1)
        b_wait(ob, 1, k + 1)
        if k + 1 < last:
            b_send(ob, 1, k + 2)
        b_spread(ob, 1, spread_after(k + 1))

    if last > 0:
        out_step(0)
    arrived(ssr, pair_recv.at[0])
    square = (ssb[yl] + ssr[...]) * (1.0 / (2 * tile_blocks * width))
    inverse = lax.rsqrt(square[:, :1] + RMS_EPS)
    arrived(qr, pair_recv.at[1])
    got = (got + qr[...].astype(f32)) * inverse
    cosine, sine = cos_ref[...], sin_ref[...]
    size = cosine.shape[1]
    heads = wq.shape[1] // size

    def rotated(v):
        return (v * cosine + pltpu.roll(v, size // 2, 1) * sine).astype(bf16).astype(f32)

    for h in range(heads):
        q = rotated(got[:, h * size:(h + 1) * size])
        for s in range(2):
            q3[:, s * heads + h, :] = q[s * rows:(s + 1) * rows]
    k_new = rotated(got[:, heads * size:(heads + 1) * size])
    v_new = got[:, (heads + 1) * size:(heads + 2) * size].astype(bf16).astype(f32)
    if last > 1:
        out_step(1)

    key_load.wait()
    value_load.wait()
    scale = size ** -0.5
    slots = kc.shape[1]
    lane = lax.broadcasted_iota(jnp.int32, (CHUNK, 2 * heads, slots), 2)
    step_of = lax.broadcasted_iota(jnp.int32, (CHUNK, 2 * heads, 1), 1)
    for r0 in range(0, rows, CHUNK):
        if r0 == rows // 2 and last > 2:
            out_step(2)
        part = slice(r0, r0 + CHUNK)
        q = q3[part]
        scores = lax.dot_general(
            q.astype(bf16), kc[part], (((2,), (2,)), ((0,), (0,))), preferred_element_type=f32
        ) * scale
        live = live_ref[part][:, None, :]
        scores = jnp.where(lane < live, scores, -jnp.inf)
        k0, k1 = k_new[r0:r0 + CHUNK][:, None, :], k_new[rows + r0:rows + r0 + CHUNK][:, None, :]
        v0, v1 = v_new[r0:r0 + CHUNK][:, None, :], v_new[rows + r0:rows + r0 + CHUNK][:, None, :]
        n0 = jnp.sum(q * k0, axis=2, keepdims=True) * scale
        n1 = jnp.sum(q * k1, axis=2, keepdims=True) * scale
        n1 = jnp.where(step_of >= heads, n1, -jnp.inf)
        top = jnp.maximum(jnp.max(scores, axis=2, keepdims=True), jnp.maximum(n0, n1))
        probs = jnp.exp(scores - top)
        e0, e1 = jnp.exp(n0 - top), jnp.exp(n1 - top)
        total = jnp.sum(probs, axis=2, keepdims=True) + e0 + e1
        mixed = lax.dot_general(
            probs.astype(bf16), vc[part], (((2,), (1,)), ((0,), (0,))), preferred_element_type=f32
        )
        mixed = mixed + e0.astype(bf16).astype(f32) * v0 + e1.astype(bf16).astype(f32) * v1
        att3[part] = mixed / total
    attended = jnp.concatenate(
        [
            jnp.concatenate([att3[:, s * heads + h, :] for h in range(heads)], axis=1)
            for s in range(2)
        ],
        axis=0,
    ).astype(bf16)
    order = one_hot_rows(
        (2, NZ, 2, NX), lambda r_, z_, s_, x_: s_ * rows + r_ * half + z_ * NX + x_
    )
    attb[yl] = pick(order, attended).astype(bf16)
    send(attb.at[yl], attb.at[yl], pair_send.at[2], pair_recv.at[2], partner)

    a_wait(oa, 1, last)
    wait_spread(ob, 1)
    arrived(attb.at[1 - yl], pair_recv.at[2])
    full = attb[...].reshape(2 * both, heads * size)
    tiles = NYH // 2
    slab = NZ // tile_blocks

    def project(j):
        left = oa[pl.ds(j * slab, slab)].reshape(width, ocut)
        right = ob[pl.ds(j * slab, slab)].reshape(width, ob.shape[2])
        dims = (((1,), (1,)), ((), ()))
        return lax.dot_general(
            full[:, :ocut], left, dims, preferred_element_type=f32
        ) + lax.dot_general(full[:, ocut:], right, dims, preferred_element_type=f32)

    for i in range(tiles):
        ps[i] = project(2 * i + 1 - c).astype(bf16)
        send(ps.at[i], pr.at[i], core_send.at[i], core_recv.at[i], sib)
    for i in range(tiles):
        pk[i] = project(2 * i + c)
    for i in range(tiles):
        arrived(pr.at[i], core_recv.at[i])
        summed = (pk[i] + pr[i].astype(f32)).astype(bf16)
        for r in range(2):
            for g in range(2):
                lo = g * both + r * rows
                sp[i, r, g * rows:(g + 1) * rows, :] = summed[lo:lo + rows]
            is_self = jnp.logical_and(tiles * yl + i == yh, yl == r)
            there = dev(x, z, r, tiles * yl + i, c)
            away = remote(sp.at[i, r], rb.at[yh], y_send.at[2 * i + r], y_recv.at[yh], there)
            here = pltpu.make_async_copy(sp.at[i, r], rb.at[yh], y_recv.at[yh])
            pl.when(jnp.logical_not(is_self))(away.start)
            pl.when(is_self)(here.start)
    result = rr[...].reshape(both, width).astype(f32)
    for k in range(NYH):
        arrived(rb.at[k], y_recv.at[k])
        result = result + rb[k].astype(f32)

    result = result.reshape(2, NZ, 2 * NX, width)
    for k in range(NZ):
        zs[k] = jnp.concatenate([result[0, k], result[1, k]], axis=0).astype(bf16)
    zr[z] = zs[z]
    for d in range(1, NZ):
        zz = lax.rem(z + d, NZ)
        send(zs.at[zz], zr.at[z], za_send.at[d - 1], za_recv.at[d - 1], dev(x, zz, yl, yh, c))
    for d in range(1, NZ):
        arrived(zr.at[lax.rem(z + NZ - d, NZ)], za_recv.at[d - 1])
    order = one_hot_rows(
        (NX, 2, NZ, 2), lambda x_, g_, z_, s_: ((z_ * 2 + g_) * 2 + s_) * NX + x_
    )
    moved = pick(order, zr[...].reshape(both, width)).astype(bf16)
    xo[...] = moved.reshape(NX, 4 * NZ, width)
    xr[x] = xo[x]
    for d in range(1, NX):
        xx = lax.rem(x + d, NX)
        send(xo.at[xx], xr.at[x], xa_send.at[d - 1], xa_recv.at[d - 1], dev(xx, z, yl, yh, c))
    for d in range(1, NX):
        arrived(xr.at[lax.rem(x + NX - d, NX)], xa_recv.at[d - 1])
    order = one_hot_rows(
        (2, NZ, NX, 2), lambda g_, z_, x_, s_: ((x_ * 2 + g_) * NZ + z_) * 2 + s_
    )
    out[...] = pick(order, xr[...].reshape(both, width)).astype(bf16)

    for copy in sent:
        copy.wait_send()
    for s, buf in ((0, wb), (1, ob)):
        for d in range(1, NX):
            view = buf.at[:, mine]
            remote(view, view, bx_send.at[s, d - 1], bx_recv.at[s, d - 1], sib).wait_send()
    for k in range(NYH):
        is_self = jnp.logical_and(yl_to == yl, yh == k)
        away = remote(xs, xg.at[yl, tile_me], xs_send.at[k], xs_recv.at[src_me], sib)
        pl.when(jnp.logical_not(is_self))(away.wait_send)
        i, r = k // 2, k % 2
        is_self = jnp.logical_and(tiles * yl + i == yh, yl == r)
        away = remote(sp.at[i, r], rb.at[yh], y_send.at[k], y_recv.at[yh], sib)
        pl.when(jnp.logical_not(is_self))(away.wait_send)


def on_device(
    hidden, next_hidden, gain, w_query, w_key, w_value, w_out,
    key_cache, value_cache, lengths, positions,
):
    rows, width = hidden.shape
    both = 2 * rows
    slots, size = key_cache.shape[2], key_cache.shape[3]
    block, qcols = w_query.shape
    heads = qcols // size
    columns = qcols + 2 * size
    cut, ocut = columns // 2, qcols // 2
    half_width = NYH * width

    lane = jnp.arange(size, dtype=jnp.int32)
    place = (lane % (size // 2)).astype(f32)
    freqs = ROPE_BASE ** (-(2.0 * place) / size)
    where_at = jnp.concatenate([positions, positions + 1]).astype(f32)
    angle = where_at[:, None] * freqs[None, :]
    cosine = jnp.cos(angle)
    sine = jnp.sin(angle) * jnp.where(lane < size // 2, -1.0, 1.0)
    live = jnp.broadcast_to(lengths[:, None], (rows, slots))
    wide_gain = gain.astype(f32).reshape(2 * NYH, 1, width)

    vmem = pl.BlockSpec(memory_space=pltpu.VMEM)
    hbm = pl.BlockSpec(memory_space=pl.ANY)
    dma = lambda *shape: pltpu.SemaphoreType.DMA(shape)
    steps = NZ // 2
    result = pl.pallas_call(
        layer_kernel,
        out_shape=jax.ShapeDtypeStruct((both, width), bf16),
        in_specs=[vmem] * 10 + [hbm] * 2,
        out_specs=vmem,
        scratch_shapes=[
            pltpu.VMEM((NZ, NX * block, cut), bf16),
            pltpu.VMEM((NZ, NX * block, columns - cut), bf16),
            pltpu.VMEM((NZ, NX * block, ocut), bf16),
            pltpu.VMEM((NZ, NX * block, qcols - ocut), bf16),
            pltpu.VMEM((both, width), bf16),
            pltpu.VMEM((2, NYH, both, width), bf16),
            pltpu.VMEM((2, both, half_width), bf16),
            pltpu.VMEM((2, both, 128), f32),
            pltpu.VMEM((both, 128), f32),
            pltpu.VMEM((both, columns), bf16),
            pltpu.VMEM((both, columns), bf16),
            pltpu.VMEM((rows, slots, size), bf16),
            pltpu.VMEM((rows, slots, size), bf16),
            pltpu.VMEM((rows, 2 * heads, size), f32),
            pltpu.VMEM((rows, 2 * heads, size), f32),
            pltpu.VMEM((2, both, qcols), bf16),
            pltpu.VMEM((NYH // 2, 2 * both, width), bf16),
            pltpu.VMEM((NYH // 2, 2 * both, width), bf16),
            pltpu.VMEM((NYH // 2, 2 * both, width), f32),
            pltpu.VMEM((NYH // 2, 2, both, width), bf16),
            pltpu.VMEM((NYH, both, width), bf16),
            pltpu.VMEM((2, rows, width), bf16),
            pltpu.VMEM((NZ, 4 * NX, width), bf16),
            pltpu.VMEM((NZ, 4 * NX, width), bf16),
            pltpu.VMEM((NX, 4 * NZ, width), bf16),
            pltpu.VMEM((NX, 4 * NZ, width), bf16),
            dma(2),
            dma(NYH), dma(NYH), dma(NYH), dma(NYH), dma(2), dma(2),
            dma(2, NX - 1), dma(2, NX - 1), dma(2, 2, steps), dma(2, 2, steps),
            dma(2, NX - 1), dma(2, NX - 1), dma(2, 2, steps), dma(2, 2, steps),
            dma(3), dma(3), dma(NYH // 2), dma(NYH // 2), dma(NYH), dma(NYH),
            dma(NZ - 1), dma(NZ - 1), dma(NX - 1), dma(NX - 1),
        ],
        compiler_params=pltpu.CompilerParams(
            collective_id=0, has_side_effects=True, vmem_limit_bytes=56 * 1024 * 1024
        ),
        name="gathered_layer",
    )(
        hidden, next_hidden, wide_gain, w_query, w_key, w_value, w_out.T,
        cosine, sine, live,
        key_cache.reshape(rows, slots, size), value_cache.reshape(rows, slots, size),
    )
    return result.reshape(rows, 2, 1, width)


def solution(mesh):
    placed = (
        P("fsdp", "tp"),
        P("fsdp", "tp"),
        P(),
        P("fsdp", "tp"),
        P("fsdp", "tp"),
        P("fsdp", "tp"),
        P("tp", "fsdp"),
        P("fsdp", "tp", None, None),
        P("fsdp", "tp", None, None),
        P("fsdp"),
        P("fsdp"),
    )
    return jax.shard_map(
        on_device,
        mesh=mesh,
        in_specs=placed,
        out_specs=P(None, None, "fsdp", "tp"),
        check_vma=False,
    )
```

```python
import functools

import jax
import jax.numpy as jnp
from jax import lax
from jax.experimental import pallas as pl
from jax.experimental.pallas import tpu as pltpu
from jax.sharding import PartitionSpec as P
import numpy as np

RMS_EPS = 1e-06
ROPE_BASE = 1000000.0
MESH = pl.DeviceIdType.MESH
NX, NZ, NYH = 4, 8, 4
CHUNK = 16

f32, bf16 = jnp.float32, jnp.bfloat16


def one_hot_rows(out_dims, source_of):
    count = 1
    for size in out_dims:
        count *= size
    row = lax.broadcasted_iota(jnp.int32, (count, count), 0)
    column = lax.broadcasted_iota(jnp.int32, (count, count), 1)
    digits, shift = [], 0
    for size in reversed(out_dims):
        bits = size.bit_length() - 1
        digits.append(lax.shift_right_logical(row, shift) & (size - 1))
        shift += bits
    digits.reverse()
    return jnp.where(source_of(*digits) == column, 1.0, 0.0).astype(bf16)


def pick(matrix, rows):
    return jnp.dot(matrix, rows, preferred_element_type=f32)


def layer_kernel(
    hid, nxt, gain, wq, wk, wv, wot, freq_ref, len_ref, pos_ref, kc_hbm, vc_hbm,
    out,
    wa, wb, oa, ob, xs, xg, xn, ssb, ssr, qs, qr, kc, vc, q3, att3, attb,
    ps, pr, pk, sp, fb, rb, rr, zs, zr, xo, xr,
    cache_sem, xs_send, xs_recv, sib_send, sib_recv, res_send, res_recv,
    ax_send, ax_recv, az_send, az_recv, bx_send, bx_recv, bf_send, bf_recv, bz_send, bz_recv,
    pair_send, pair_recv, core_send, core_recv, y_send, f_recv, y_recv,
    za_send, za_recv, xa_send, xa_recv,
):
    rows = hid.shape[0]
    half = rows // 2
    both = 2 * rows
    width = hid.shape[1]
    block = wq.shape[0]
    tile_blocks = NYH
    split = width // 256 * 128 + 128 if width >= 256 else width // 2
    f, t = lax.axis_index("fsdp"), lax.axis_index("tp")
    x, z, yl = lax.rem(f, NX), lax.rem(f // NX, NZ), f // (NX * NZ)
    yh, c = t // 2, lax.rem(t, 2)

    def dev(x_, z_, yl_, yh_, c_):
        return ((yl_ * NZ + z_) * NX + x_, yh_ * 2 + c_)

    def remote(src, dst, send, recv, where):
        return pltpu.make_async_remote_copy(
            src_ref=src, dst_ref=dst, send_sem=send, recv_sem=recv,
            device_id=where, device_id_type=MESH,
        )

    def arrived(dst, sem):
        pltpu.make_async_copy(dst, dst, sem).wait()

    sent = []

    def send(*args):
        copy = remote(*args)
        copy.start()
        sent.append(copy)

    key_load = pltpu.make_async_copy(kc_hbm, kc, cache_sem.at[0])
    value_load = pltpu.make_async_copy(vc_hbm, vc, cache_sem.at[1])
    key_load.start()
    value_load.start()

    y = 2 * yh + yl
    ny = 2 * NYH
    sib = dev(x, z, yl, yh, 1 - c)
    partner = dev(x, z, 1 - yl, yh, c)
    places = [dev(lax.rem(x + d, NX), z, yl, yh, c) for d in range(1, NX)]
    places += [dev(x, lax.rem(z + d, NZ), yl, yh, c) for d in range(1, NZ)]
    for d in range(1, ny):
        yy = lax.rem(y + d, ny)
        places.append(dev(x, z, lax.rem(yy, 2), yy // 2, c))
    places.append(sib)
    barrier = pltpu.get_barrier_semaphore()
    for where in places:
        pl.semaphore_signal(barrier, inc=1, device_id=where, device_id_type=MESH)

    mine = pl.ds(pl.multiple_of(x * block, block), block)
    cut = wa.shape[2]
    own = jnp.concatenate([wq[...], wk[...], wv[...]], axis=1)
    wa[z, mine, :] = own[:, :cut]
    wb[z, mine, :] = own[:, cut:]
    ocut = oa.shape[2]
    oa[z, mine, :] = wot[:, :ocut]
    ob[z, mine, :] = wot[:, ocut:]
    xs[0:rows, :] = hid[...]
    xs[rows:both, :] = nxt[...]
    pl.semaphore_wait(barrier, len(places))

    yl_to = yh // (NYH // 2)
    tile_me = lax.rem(yh, NYH // 2) * 2 + c
    src_me = yl * (NYH // 2) + lax.rem(yh, NYH // 2)
    for k in range(NYH):
        is_self = jnp.logical_and(yl_to == yl, yh == k)
        there = dev(x, z, yl_to, k, c)
        away = remote(xs, xg.at[yl, tile_me], xs_send.at[k], xs_recv.at[src_me], there)
        here = pltpu.make_async_copy(xs, xg.at[yl, tile_me], xs_recv.at[src_me])
        pl.when(jnp.logical_not(is_self))(away.start)
        pl.when(is_self)(here.start)

    up = dev(x, lax.rem(z + 1, NZ), yl, yh, c)
    down = dev(x, lax.rem(z + NZ - 1, NZ), yl, yh, c)
    last = NZ // 2 - 1

    def first_x(buf, s):
        for d in range(1, NX):
            there = dev(lax.rem(x + d, NX), z, yl, yh, c)
            send(buf.at[z, mine], buf.at[z, mine], ax_send.at[s, d - 1], ax_recv.at[s, d - 1], there)

    def wait_first_x(buf, s):
        for d in range(1, NX):
            xx = lax.rem(x + NX - d, NX)
            arrived(buf.at[z, pl.ds(pl.multiple_of(xx * block, block), block)], ax_recv.at[s, d - 1])

    def slab_parts(k):
        if k == last:
            h = NX * block // 2
            return pl.ds(0, h), pl.ds(h, h)
        return pl.ds(0, NX * block), pl.ds(0, NX * block)

    def a_send(buf, s, k):
        p_up, p_down = slab_parts(k)
        zz = lax.rem(z + NZ - k, NZ)
        send(buf.at[zz, p_up], buf.at[zz, p_up], az_send.at[s, 0, k], az_recv.at[s, 0, k], up)
        zz = lax.rem(z + k, NZ)
        send(buf.at[zz, p_down], buf.at[zz, p_down], az_send.at[s, 1, k], az_recv.at[s, 1, k], down)

    def a_wait(buf, s, k):
        p_up, p_down = slab_parts(k)
        arrived(buf.at[lax.rem(z + NZ - 1 - k, NZ), p_up], az_recv.at[s, 0, k])
        arrived(buf.at[lax.rem(z + 1 + k, NZ), p_down], az_recv.at[s, 1, k])

    def b_send(buf, s, k):
        zz = lax.rem(z + NZ - k, NZ)
        send(buf.at[zz, mine], buf.at[zz, mine], bz_send.at[s, 0, k], bz_recv.at[s, 0, k], up)
        if k < last:
            zz = lax.rem(z + k, NZ)
            send(buf.at[zz, mine], buf.at[zz, mine], bz_send.at[s, 1, k], bz_recv.at[s, 1, k], down)

    def b_wait(buf, s, k):
        arrived(buf.at[lax.rem(z + NZ - 1 - k, NZ), mine], bz_recv.at[s, 0, k])
        if k < last:
            arrived(buf.at[lax.rem(z + 1 + k, NZ), mine], bz_recv.at[s, 1, k])

    x_up, x_down = lax.rem(x + 1, NX), lax.rem(x + NX - 1, NX)
    beside = ((x_up, x_down), (x_down, x_up))[:min(2, NX - 1)]

    def column(x_):
        return pl.ds(pl.multiple_of(x_ * block, block), block)

    def place(o):
        return NZ // 2 * 2 - 1 if o == -NZ // 2 else (2 * o if o >= 0 else -2 * o - 1)

    def b_spread(buf, s, offsets):
        for o in offsets:
            view = buf.at[lax.rem(z + NZ + o, NZ), mine]
            for w, (to, _) in enumerate(beside):
                send(view, view, bx_send.at[s, w, place(o)], bx_recv.at[s, w, place(o)],
                     dev(to, z, yl, yh, c))

    def b_relay(buf, s, offsets):
        for o in offsets:
            zz = lax.rem(z + NZ + o, NZ)
            for w, (to, came) in enumerate(beside):
                view = buf.at[zz, column(came)]
                arrived(view, bx_recv.at[s, w, place(o)])
                if NX == 4 and place(o) % 2 == w:
                    send(view, view, bf_send.at[s, place(o)], bf_recv.at[s, place(o)],
                         dev(to, z, yl, yh, c))

    def spread_after(k):
        return (-1 - k,) if k == last else (-1 - k, 1 + k)

    def wait_relays(buf, s):
        if NX == 4:
            far = column(lax.rem(x + 2, NX))
            for o in range(-NZ // 2, NZ // 2):
                arrived(buf.at[lax.rem(z + NZ + o, NZ), far], bf_recv.at[s, place(o)])

    first_x(wa, 0)
    b_send(wb, 0, 0)
    b_spread(wb, 0, (0,))

    away_rows = half * (1 - yl)
    own_rows = half * yl
    for s in range(2):
        src = xs.at[pl.ds(pl.multiple_of(s * rows + away_rows, half), half)]
        send(src, rr.at[yl, pl.ds(s * half, half)], res_send.at[s], res_recv.at[s], partner)
        rr[yl, s * half:(s + 1) * half, :] = xs[pl.ds(pl.multiple_of(s * rows + own_rows, half), half), :]

    wait_first_x(wa, 0)
    a_send(wa, 0, 0)
    first_x(oa, 1)
    b_send(ob, 1, 0)
    for k in range(last):
        b_wait(wb, 0, k)
        b_send(wb, 0, k + 1)
        b_spread(wb, 0, spread_after(k))
        b_relay(wb, 0, spread_after(k - 1) if k else (0,))
        a_wait(wa, 0, k)
        a_send(wa, 0, k + 1)

    for k in range(NYH):
        slot = xg.at[k // (NYH // 2), (k % (NYH // 2)) * 2 + c]
        arrived(slot, xs_recv.at[k])
        send(slot, slot, sib_send.at[k], sib_recv.at[k], sib)
    b_wait(wb, 0, last)
    b_spread(wb, 0, spread_after(last))
    b_relay(wb, 0, spread_after(last - 1))
    for k in range(NYH):
        arrived(xg.at[k // (NYH // 2), (k % (NYH // 2)) * 2 + (1 - c)], sib_recv.at[k])

    def scale_row(j):
        start = pl.multiple_of((yl * tile_blocks + j) * width, width)
        return gain[:, pl.ds(start, width)].astype(f32)

    for g in range(2):
        total = jnp.zeros((both, 1), f32)
        for j in range(tile_blocks):
            values = xg[g, j].astype(f32)
            total = total + jnp.sum(values * values, axis=1, keepdims=True)
            xn[g, :, j * width:(j + 1) * width] = (values * scale_row(j)).astype(bf16)
        ssb[g] = jnp.broadcast_to(total, (both, 128))
    send(ssb.at[1 - yl], ssr, pair_send.at[0], pair_recv.at[0], partner)
    b_relay(wb, 0, spread_after(last))

    def as_column(row):
        grid = (rows, rows)
        diagonal = lax.broadcasted_iota(jnp.int32, grid, 0) == lax.broadcasted_iota(jnp.int32, grid, 1)
        spread = jnp.broadcast_to(row[...].astype(f32), grid)
        return jnp.sum(jnp.where(diagonal, spread, 0.0), axis=1, keepdims=True)

    size = kc.shape[2]
    first_at = as_column(pos_ref)
    angle = jnp.concatenate([first_at, first_at + 1.0], axis=0) * freq_ref[...]
    lane = lax.broadcasted_iota(jnp.int32, (both, size), 1)
    cosine = jnp.cos(angle)
    sine = jnp.where(lane < size // 2, -1.0, 1.0) * jnp.sin(angle)
    live_rows = jnp.broadcast_to(as_column(len_ref), (rows, kc.shape[1]))

    for s in range(2):
        arrived(rr.at[1 - yl, pl.ds(s * half, half)], res_recv.at[s])
    order = one_hot_rows((NZ, 2, NX), lambda z_, s_, x_: s_ * half + z_ * NX + x_)
    for g in range(2):
        rr[g] = pick(order, rr[g]).astype(bf16)

    a_wait(wa, 0, last)
    wait_relays(wb, 0)
    wait_first_x(oa, 1)
    a_send(oa, 1, 0)
    b_spread(ob, 1, (0,))
    b_wait(ob, 1, 0)
    b_send(ob, 1, 1)
    b_spread(ob, 1, spread_after(0))
    depth = NZ * NX * block
    weight_a = wa[...].reshape(depth, cut)
    weight_b = wb[...].reshape(depth, wb.shape[2])
    theirs = xn[1 - yl]
    qs[:, :cut] = jnp.dot(theirs, weight_a, preferred_element_type=f32).astype(bf16)
    qs[:, cut:] = jnp.dot(theirs, weight_b, preferred_element_type=f32).astype(bf16)
    send(qs, qr, pair_send.at[1], pair_recv.at[1], partner)
    b_relay(ob, 1, (0,))
    ours = xn[yl]
    got_a = jnp.dot(ours, weight_a, preferred_element_type=f32)
    got_b = jnp.dot(ours, weight_b, preferred_element_type=f32)
    got = jnp.concatenate([got_a, got_b], axis=1)

    def out_step(k):
        a_wait(oa, 1, k)
        a_send(oa, 1, k + 1)
        b_wait(ob, 1, k + 1)
        if k + 1 < last:
            b_send(ob, 1, k + 2)
        b_spread(ob, 1, spread_after(k + 1))
        b_relay(ob, 1, spread_after(k))

    if last > 0:
        out_step(0)
    arrived(ssr, pair_recv.at[0])
    square = (ssb[yl] + ssr[...]) * (1.0 / (2 * tile_blocks * width))
    inverse = lax.rsqrt(square[:, :1] + RMS_EPS)
    arrived(qr, pair_recv.at[1])
    got = (got + qr[...].astype(f32)) * inverse
    heads = wq.shape[1] // size

    def rotated(v):
        return (v * cosine + pltpu.roll(v, size // 2, 1) * sine).astype(bf16).astype(f32)

    for h in range(heads):
        q = rotated(got[:, h * size:(h + 1) * size])
        for s in range(2):
            q3[:, s * heads + h, :] = q[s * rows:(s + 1) * rows]
    k_new = rotated(got[:, heads * size:(heads + 1) * size])
    v_new = got[:, (heads + 1) * size:(heads + 2) * size].astype(bf16).astype(f32)
    if last > 1:
        out_step(1)

    key_load.wait()
    value_load.wait()
    scale = size ** -0.5
    slots = kc.shape[1]
    lane = lax.broadcasted_iota(jnp.int32, (CHUNK, 2 * heads, slots), 2).astype(f32)
    step_of = lax.broadcasted_iota(jnp.int32, (CHUNK, 2 * heads, 1), 1)
    for r0 in range(0, rows, CHUNK):
        if r0 == rows // 2 and last > 2:
            out_step(2)
        part = slice(r0, r0 + CHUNK)
        q = q3[part]
        scores = lax.dot_general(
            q.astype(bf16), kc[part], (((2,), (2,)), ((0,), (0,))), preferred_element_type=f32
        ) * scale
        live = live_rows[part][:, None, :]
        scores = jnp.where(lane < live, scores, -jnp.inf)
        k0, k1 = k_new[r0:r0 + CHUNK][:, None, :], k_new[rows + r0:rows + r0 + CHUNK][:, None, :]
        v0, v1 = v_new[r0:r0 + CHUNK][:, None, :], v_new[rows + r0:rows + r0 + CHUNK][:, None, :]
        n0 = jnp.sum(q * k0, axis=2, keepdims=True) * scale
        n1 = jnp.sum(q * k1, axis=2, keepdims=True) * scale
        n1 = jnp.where(step_of >= heads, n1, -jnp.inf)
        top = jnp.maximum(jnp.max(scores, axis=2, keepdims=True), jnp.maximum(n0, n1))
        probs = jnp.exp(scores - top)
        e0, e1 = jnp.exp(n0 - top), jnp.exp(n1 - top)
        total = jnp.sum(probs, axis=2, keepdims=True) + e0 + e1
        mixed = lax.dot_general(
            probs.astype(bf16), vc[part], (((2,), (1,)), ((0,), (0,))), preferred_element_type=f32
        )
        mixed = mixed + e0.astype(bf16).astype(f32) * v0 + e1.astype(bf16).astype(f32) * v1
        att3[part] = mixed / total
    attended = jnp.concatenate(
        [
            jnp.concatenate([att3[:, s * heads + h, :] for h in range(heads)], axis=1)
            for s in range(2)
        ],
        axis=0,
    ).astype(bf16)
    order = one_hot_rows(
        (2, NZ, 2, NX), lambda r_, z_, s_, x_: s_ * rows + r_ * half + z_ * NX + x_
    )
    attb[yl] = pick(order, attended).astype(bf16)
    send(attb.at[yl], attb.at[yl], pair_send.at[2], pair_recv.at[2], partner)

    b_relay(ob, 1, spread_after(last))
    a_wait(oa, 1, last)
    wait_relays(ob, 1)
    arrived(attb.at[1 - yl], pair_recv.at[2])
    full = attb[...].reshape(2 * both, heads * size)
    tiles = NYH // 2
    slab = NZ // tile_blocks

    def project(j):
        left = oa[pl.ds(j * slab, slab)].reshape(width, ocut)
        right = ob[pl.ds(j * slab, slab)].reshape(width, ob.shape[2])
        dims = (((1,), (1,)), ((), ()))
        return lax.dot_general(
            full[:, :ocut], left, dims, preferred_element_type=f32
        ) + lax.dot_general(full[:, ocut:], right, dims, preferred_element_type=f32)

    for i in range(tiles):
        ps[i] = project(2 * i + 1 - c).astype(bf16)
        send(ps.at[i], pr.at[i], core_send.at[i], core_recv.at[i], sib)
    for i in range(tiles):
        pk[i] = project(2 * i + c)
    for i in range(tiles):
        arrived(pr.at[i], core_recv.at[i])
        summed = (pk[i] + pr[i].astype(f32)).astype(bf16)
        for r in range(2):
            for g in range(2):
                lo = g * both + r * rows
                sp[2 * i + r, g * rows:(g + 1) * rows, :] = summed[lo:lo + rows]

    def at(yy):
        yy = lax.rem(yy + ny, ny)
        return dev(x, z, lax.rem(yy, 2), yy // 2, c)

    def ahead(m):
        return lax.rem(NYH * yl + m - y + 2 * ny, ny)

    cuts = [pl.ds(0, split), pl.ds(split, width - split)]

    def either(delta, *values):
        hit = delta == values[0]
        for value in values[1:]:
            hit = jnp.logical_or(hit, delta == value)
        return hit

    def far_copy(m, h, to):
        return remote(sp.at[m, :, cuts[h]], fb.at[m, :, cuts[h]], y_send.at[m, h], f_recv.at[m, h], to)

    def near_copy(m, h, side, to):
        return remote(sp.at[m, :, cuts[h]], rb.at[side, :, cuts[h]], y_send.at[m, h], y_recv.at[side, h], to)

    for h in range(2):
        for m in range(NYH):
            delta = ahead(m)
            pl.when(either(delta, 3, 4) if h == 0 else delta == 3)(far_copy(m, h, at(y + 2)).start)
            pl.when(delta == 5 if h == 0 else either(delta, 4, 5))(far_copy(m, h, at(y - 2)).start)
    for h in range(2):
        for m in range(NYH):
            delta = ahead(m)

            @pl.when(either(delta, 1, 7, 2 if h == 0 else 6))
            def _():
                arrived(fb.at[m, :, cuts[h]], f_recv.at[m, h])
                lanes = slice(0, split) if h == 0 else slice(split, width)
                sp[m, :, lanes] = (sp[m, :, lanes].astype(f32) + fb[m, :, lanes].astype(f32)).astype(bf16)

            pl.when(either(delta, 1, 2))(near_copy(m, h, 0, at(NYH * yl + m)).start)
            pl.when(either(delta, 6, 7))(near_copy(m, h, 1, at(NYH * yl + m)).start)

    holds = jnp.where(y // NYH == yl, 1.0, 0.0)
    for h in range(2):
        lanes = slice(0, split) if h == 0 else slice(split, width)
        result = rr[:, :, lanes].reshape(both, -1).astype(f32)
        result = result + sp[lax.rem(y, NYH), :, lanes].astype(f32) * holds
        for side in range(2):
            arrived(rb.at[side, :, cuts[h]], y_recv.at[side, h])
            result = result + rb[side, :, lanes].astype(f32)
        result = result.reshape(2, NZ, 2 * NX, result.shape[1])
        for k in range(NZ):
            zs[k, :, lanes] = jnp.concatenate([result[0, k], result[1, k]], axis=0).astype(bf16)
        zr[z, :, lanes] = zs[z, :, lanes]
        for d in range(1, NZ):
            zz = lax.rem(z + d, NZ)
            send(zs.at[zz, :, cuts[h]], zr.at[z, :, cuts[h]], za_send.at[h, d - 1], za_recv.at[h, d - 1],
                 dev(x, zz, yl, yh, c))
    order = one_hot_rows(
        (NX, 2, NZ, 2), lambda x_, g_, z_, s_: ((z_ * 2 + g_) * 2 + s_) * NX + x_
    )
    for h in range(2):
        lanes = slice(0, split) if h == 0 else slice(split, width)
        for d in range(1, NZ):
            arrived(zr.at[lax.rem(z + NZ - d, NZ), :, cuts[h]], za_recv.at[h, d - 1])
        moved = pick(order, zr[:, :, lanes].reshape(both, -1)).astype(bf16)
        xo[:, :, lanes] = moved.reshape(NX, 4 * NZ, moved.shape[1])
        xr[x, :, lanes] = xo[x, :, lanes]
        for d in range(1, NX):
            xx = lax.rem(x + d, NX)
            send(xo.at[xx, :, cuts[h]], xr.at[x, :, cuts[h]], xa_send.at[h, d - 1], xa_recv.at[h, d - 1],
                 dev(xx, z, yl, yh, c))
    order = one_hot_rows(
        (2, NZ, NX, 2), lambda g_, z_, x_, s_: ((x_ * 2 + g_) * NZ + z_) * 2 + s_
    )
    for h in range(2):
        lanes = slice(0, split) if h == 0 else slice(split, width)
        for d in range(1, NX):
            arrived(xr.at[lax.rem(x + NX - d, NX), :, cuts[h]], xa_recv.at[h, d - 1])
        out[:, lanes] = pick(order, xr[:, :, lanes].reshape(both, -1)).astype(bf16)

    for copy in sent:
        copy.wait_send()
    for k in range(NYH):
        is_self = jnp.logical_and(yl_to == yl, yh == k)
        away = remote(xs, xg.at[yl, tile_me], xs_send.at[k], xs_recv.at[src_me], sib)
        pl.when(jnp.logical_not(is_self))(away.wait_send)
        for h in range(2):
            pl.when(ahead(k) != 0)(far_copy(k, h, sib).wait_send)


def on_device(
    hidden, next_hidden, gain, w_query, w_key, w_value, w_out,
    key_cache, value_cache, lengths, positions,
):
    rows, width = hidden.shape
    both = 2 * rows
    slots, size = key_cache.shape[2], key_cache.shape[3]
    block, qcols = w_query.shape
    heads = qcols // size
    columns = qcols + 2 * size
    cut, ocut = columns // 2, qcols // 2
    half_width = NYH * width

    place = np.arange(size) % (size // 2)
    freqs = (ROPE_BASE ** (-(2.0 * place) / size)).astype(np.float32)[None, :]

    vmem = pl.BlockSpec(memory_space=pltpu.VMEM)
    hbm = pl.BlockSpec(memory_space=pl.ANY)
    dma = lambda *shape: pltpu.SemaphoreType.DMA(shape)
    steps = NZ // 2
    result = pl.pallas_call(
        layer_kernel,
        out_shape=jax.ShapeDtypeStruct((both, width), bf16),
        in_specs=[vmem] * 10 + [hbm] * 2,
        out_specs=vmem,
        scratch_shapes=[
            pltpu.VMEM((NZ, NX * block, cut), bf16),
            pltpu.VMEM((NZ, NX * block, columns - cut), bf16),
            pltpu.VMEM((NZ, NX * block, ocut), bf16),
            pltpu.VMEM((NZ, NX * block, qcols - ocut), bf16),
            pltpu.VMEM((both, width), bf16),
            pltpu.VMEM((2, NYH, both, width), bf16),
            pltpu.VMEM((2, both, half_width), bf16),
            pltpu.VMEM((2, both, 128), f32),
            pltpu.VMEM((both, 128), f32),
            pltpu.VMEM((both, columns), bf16),
            pltpu.VMEM((both, columns), bf16),
            pltpu.VMEM((rows, slots, size), bf16),
            pltpu.VMEM((rows, slots, size), bf16),
            pltpu.VMEM((rows, 2 * heads, size), f32),
            pltpu.VMEM((rows, 2 * heads, size), f32),
            pltpu.VMEM((2, both, qcols), bf16),
            pltpu.VMEM((NYH // 2, 2 * both, width), bf16),
            pltpu.VMEM((NYH // 2, 2 * both, width), bf16),
            pltpu.VMEM((NYH // 2, 2 * both, width), f32),
            pltpu.VMEM((NYH, both, width), bf16),
            pltpu.VMEM((NYH, both, width), bf16),
            pltpu.VMEM((2, both, width), bf16),
            pltpu.VMEM((2, rows, width), bf16),
            pltpu.VMEM((NZ, 4 * NX, width), bf16),
            pltpu.VMEM((NZ, 4 * NX, width), bf16),
            pltpu.VMEM((NX, 4 * NZ, width), bf16),
            pltpu.VMEM((NX, 4 * NZ, width), bf16),
            dma(2),
            dma(NYH), dma(NYH), dma(NYH), dma(NYH), dma(2), dma(2),
            dma(2, NX - 1), dma(2, NX - 1), dma(2, 2, steps), dma(2, 2, steps),
            dma(2, 2, NZ), dma(2, 2, NZ), dma(2, NZ), dma(2, NZ), dma(2, 2, steps), dma(2, 2, steps),
            dma(3), dma(3), dma(NYH // 2), dma(NYH // 2), dma(NYH, 2), dma(NYH, 2), dma(2, 2),
            dma(2, NZ - 1), dma(2, NZ - 1), dma(2, NX - 1), dma(2, NX - 1),
        ],
        compiler_params=pltpu.CompilerParams(
            collective_id=0, has_side_effects=True, vmem_limit_bytes=56 * 1024 * 1024
        ),
        name="gathered_layer",
    )(
        hidden, next_hidden, gain[None, :], w_query, w_key, w_value, w_out.T,
        jnp.asarray(freqs), lengths[None, :], positions[None, :],
        key_cache.reshape(rows, slots, size), value_cache.reshape(rows, slots, size),
    )
    return result.reshape(rows, 2, 1, width)


def solution(mesh):
    placed = (
        P("fsdp", "tp"),
        P("fsdp", "tp"),
        P(),
        P("fsdp", "tp"),
        P("fsdp", "tp"),
        P("fsdp", "tp"),
        P("tp", "fsdp"),
        P("fsdp", "tp", None, None),
        P("fsdp", "tp", None, None),
        P("fsdp"),
        P("fsdp"),
    )
    return jax.shard_map(
        on_device,
        mesh=mesh,
        in_specs=placed,
        out_specs=P(None, None, "fsdp", "tp"),
        check_vma=False,
    )
```

```python
import functools

import jax
import jax.numpy as jnp
from jax import lax
from jax.experimental import pallas as pl
from jax.experimental.pallas import tpu as pltpu
from jax.sharding import PartitionSpec as P
import numpy as np

RMS_EPS = 1e-06
ROPE_BASE = 1000000.0
MESH = pl.DeviceIdType.MESH
NX, NZ, NYH = 4, 8, 4
CHUNK = 16

f32, bf16 = jnp.float32, jnp.bfloat16


def one_hot_rows(out_dims, source_of):
    count = 1
    for size in out_dims:
        count *= size
    row = lax.broadcasted_iota(jnp.int32, (count, count), 0)
    column = lax.broadcasted_iota(jnp.int32, (count, count), 1)
    digits, shift = [], 0
    for size in reversed(out_dims):
        bits = size.bit_length() - 1
        digits.append(lax.shift_right_logical(row, shift) & (size - 1))
        shift += bits
    digits.reverse()
    return jnp.where(source_of(*digits) == column, 1.0, 0.0).astype(bf16)


def pick(matrix, rows):
    return jnp.dot(matrix, rows, preferred_element_type=f32)


def layer_kernel(
    hid, nxt, gain, wq, wk, wv, wot, freq_ref, len_ref, pos_ref, kc_hbm, vc_hbm,
    out,
    wa, wb, oa, ob, xs, xg, xn, wide, ssb, ssr, qs, qr, kc, vc, q3, att3, attb,
    ps, pr, sp, fb, rb, rr, zs, zr, xo, xr,
    cache_sem, xs_send, xs_recv, sib_send, sib_recv, res_send, res_recv,
    ax_send, ax_recv, az_send, az_recv, bx_send, bx_recv, bz_send, bz_recv,
    pair_send, pair_recv, core_send, core_recv, y_send, f_recv, y_recv,
    za_send, za_recv, xa_send, xa_recv,
):
    rows = hid.shape[0]
    half = rows // 2
    both = 2 * rows
    width = hid.shape[1]
    block = wq.shape[0]
    tile_blocks = NYH
    split = width // 256 * 128 + 128 if width >= 256 else width // 2
    f, t = lax.axis_index("fsdp"), lax.axis_index("tp")
    x, z, yl = lax.rem(f, NX), lax.rem(f // NX, NZ), f // (NX * NZ)
    yh, c = t // 2, lax.rem(t, 2)

    def dev(x_, z_, yl_, yh_, c_):
        return ((yl_ * NZ + z_) * NX + x_, yh_ * 2 + c_)

    def remote(src, dst, send, recv, where):
        return pltpu.make_async_remote_copy(
            src_ref=src, dst_ref=dst, send_sem=send, recv_sem=recv,
            device_id=where, device_id_type=MESH,
        )

    def arrived(dst, sem):
        pltpu.make_async_copy(dst, dst, sem).wait()

    sent = []

    def send(*args):
        copy = remote(*args)
        copy.start()
        sent.append(copy)

    key_load = pltpu.make_async_copy(kc_hbm, kc, cache_sem.at[0])
    value_load = pltpu.make_async_copy(vc_hbm, vc, cache_sem.at[1])
    key_load.start()
    value_load.start()

    y = 2 * yh + yl
    ny = 2 * NYH
    sib = dev(x, z, yl, yh, 1 - c)
    partner = dev(x, z, 1 - yl, yh, c)
    places = [dev(lax.rem(x + d, NX), z, yl, yh, c) for d in range(1, NX)]
    places += [dev(x, lax.rem(z + d, NZ), yl, yh, c) for d in range(1, NZ)]
    for d in range(1, ny):
        yy = lax.rem(y + d, ny)
        places.append(dev(x, z, lax.rem(yy, 2), yy // 2, c))
    places.append(sib)
    barrier = pltpu.get_barrier_semaphore()
    for where in places:
        pl.semaphore_signal(barrier, inc=1, device_id=where, device_id_type=MESH)

    mine = pl.ds(pl.multiple_of(x * block, block), block)
    cut = wa.shape[2]
    own = jnp.concatenate([wq[...], wk[...], wv[...]], axis=1)
    wa[z, mine, :] = own[:, :cut]
    wb[z, mine, :] = own[:, cut:]
    ocut = oa.shape[2]
    oa[z, mine, :] = wot[:, :ocut]
    ob[z, mine, :] = wot[:, ocut:]
    xs[0:rows, :] = hid[...]
    xs[rows:both, :] = nxt[...]
    pl.semaphore_wait(barrier, len(places))

    yl_to = yh // (NYH // 2)
    tile_me = lax.rem(yh, NYH // 2) * 2 + c
    src_me = yl * (NYH // 2) + lax.rem(yh, NYH // 2)
    for k in range(NYH):
        is_self = jnp.logical_and(yl_to == yl, yh == k)
        there = dev(x, z, yl_to, k, c)
        away = remote(xs, xg.at[yl, tile_me], xs_send.at[k], xs_recv.at[src_me], there)
        here = pltpu.make_async_copy(xs, xg.at[yl, tile_me], xs_recv.at[src_me])
        pl.when(jnp.logical_not(is_self))(away.start)
        pl.when(is_self)(here.start)

    up = dev(x, lax.rem(z + 1, NZ), yl, yh, c)
    down = dev(x, lax.rem(z + NZ - 1, NZ), yl, yh, c)
    last = NZ // 2 - 1

    turns = tuple(range(NX)) if NX < 4 else (0, 1, 3, 2)

    def column(e):
        return pl.ds(pl.multiple_of(lax.rem(x + e, NX) * block, block), block)

    def plane(o):
        return lax.rem(z + NZ + o, NZ)

    def first_x(buf, s):
        for d in range(1, NX):
            there = dev(lax.rem(x + d, NX), z, yl, yh, c)
            send(buf.at[z, mine], buf.at[z, mine], ax_send.at[s, d - 1], ax_recv.at[s, d - 1], there)

    def carried(k, w, i):
        return k < last or (i < NX // 2) == (w == 0)

    def a_send(buf, s, k, i):
        for w, (to, zz) in enumerate(((up, plane(-k)), (down, plane(k)))):
            if carried(k, w, i):
                view = buf.at[zz, column(turns[i])]
                send(view, view, az_send.at[s, w, k, i], az_recv.at[s, w, k, i], to)

    def a_wait(buf, s, k, i):
        for w, zz in enumerate((plane(-1 - k), plane(1 + k))):
            if carried(k, w, i):
                arrived(buf.at[zz, column(turns[i])], az_recv.at[s, w, k, i])

    def b_send(buf, s, k):
        for w, (to, zz) in enumerate(((up, plane(-k)), (down, plane(k)))):
            if k < last or w == 0:
                send(buf.at[zz, mine], buf.at[zz, mine], bz_send.at[s, w, k], bz_recv.at[s, w, k], to)

    def b_wait(buf, s, k):
        for w, zz in enumerate((plane(-1 - k), plane(1 + k))):
            if k < last or w == 0:
                arrived(buf.at[zz, mine], bz_recv.at[s, w, k])

    def b_spread(buf, s, offsets):
        for o in offsets:
            for d in range(1, NX):
                there = dev(lax.rem(x + d, NX), z, yl, yh, c)
                view = buf.at[plane(o), mine]
                remote(view, view, bx_send.at[s, d - 1], bx_recv.at[s, d - 1], there).start()

    def wait_spread(buf, s):
        for d in range(1, NX):
            arrived(buf.at[:, column(NX - d)], bx_recv.at[s, d - 1])

    def stream(a_buf, b_buf, s):
        def start():
            a_send(a_buf, s, 0, 0)
            b_send(b_buf, s, 0)
            first_x(a_buf, s)
            b_spread(b_buf, s, (0,))

        def from_x(i):
            arrived(a_buf.at[z, column(turns[i])], ax_recv.at[s, NX - turns[i] - 1])
            a_send(a_buf, s, 0, i)

        def b_step(k):
            b_wait(b_buf, s, k)
            if k < last:
                b_send(b_buf, s, k + 1)
            b_spread(b_buf, s, (-1 - k,) if k == last else (-1 - k, 1 + k))

        def a_step(k, i):
            a_wait(a_buf, s, k, i)
            a_send(a_buf, s, k + 1, i)

        steps = [start]
        steps += [functools.partial(from_x, i) for i in range(1, NX)]
        for k in range(last + 1):
            steps.append(functools.partial(b_step, k))
            if k < last:
                steps += [functools.partial(a_step, k, i) for i in range(NX)]
        return steps

    def stream_end(a_buf, b_buf, s):
        for i in range(NX):
            a_wait(a_buf, s, last, i)
        wait_spread(b_buf, s)

    out_steps = stream(oa, ob, 1)

    def pump(count):
        for _ in range(min(count, len(out_steps))):
            out_steps.pop(0)()

    in_steps = stream(wa, wb, 0)
    in_steps.pop(0)()

    away_rows = half * (1 - yl)
    own_rows = half * yl
    for s in range(2):
        src = xs.at[pl.ds(pl.multiple_of(s * rows + away_rows, half), half)]
        send(src, rr.at[yl, pl.ds(s * half, half)], res_send.at[s], res_recv.at[s], partner)
        rr[yl, s * half:(s + 1) * half, :] = xs[pl.ds(pl.multiple_of(s * rows + own_rows, half), half), :]

    def as_column(row):
        grid = (rows, rows)
        diagonal = lax.broadcasted_iota(jnp.int32, grid, 0) == lax.broadcasted_iota(jnp.int32, grid, 1)
        spread = jnp.broadcast_to(row[...].astype(f32), grid)
        return jnp.sum(jnp.where(diagonal, spread, 0.0), axis=1, keepdims=True)

    size = kc.shape[2]
    for step in in_steps:
        step()

    for k in range(NYH):
        slot = xg.at[k // (NYH // 2), (k % (NYH // 2)) * 2 + c]
        arrived(slot, xs_recv.at[k])
        send(slot, slot, sib_send.at[k], sib_recv.at[k], sib)
    pump(1)
    for k in range(NYH):
        arrived(xg.at[k // (NYH // 2), (k % (NYH // 2)) * 2 + (1 - c)], sib_recv.at[k])

    wide[...] = gain[...].astype(f32)
    piece = min(128, width)
    for g in range(2):
        total = jnp.zeros((both, 1), f32)
        for j in range(tile_blocks):
            values = xg[g, j].astype(f32)
            total = total + jnp.sum(values * values, axis=1, keepdims=True)
            for p in range(width // piece):
                row = (yl * tile_blocks + j) * (width // piece) + p
                xn[g, :, j * width + p * piece:j * width + (p + 1) * piece] = (
                    values[:, p * piece:(p + 1) * piece] * wide[pl.ds(row, 1), :]
                ).astype(bf16)
        ssb[g] = jnp.broadcast_to(total, (both, 128))
    send(ssb.at[1 - yl], ssr, pair_send.at[0], pair_recv.at[0], partner)
    pump(2)

    first_at = as_column(pos_ref)
    angle = jnp.concatenate([first_at, first_at + 1.0], axis=0) * freq_ref[...]
    lane = lax.broadcasted_iota(jnp.int32, (both, size), 1)
    cosine = jnp.cos(angle)
    sine = jnp.where(lane < size // 2, -1.0, 1.0) * jnp.sin(angle)
    live_rows = jnp.broadcast_to(as_column(len_ref), (rows, kc.shape[1]))

    for s in range(2):
        arrived(rr.at[1 - yl, pl.ds(s * half, half)], res_recv.at[s])
    order = one_hot_rows((NZ, 2, NX), lambda z_, s_, x_: s_ * half + z_ * NX + x_)
    for g in range(2):
        rr[g] = pick(order, rr[g]).astype(bf16)

    pump(1)
    stream_end(wa, wb, 0)
    depth = NZ * NX * block
    weight_a = wa[...].reshape(depth, cut)
    weight_b = wb[...].reshape(depth, wb.shape[2])
    theirs = xn[1 - yl]
    qs[:, :cut] = jnp.dot(theirs, weight_a, preferred_element_type=f32).astype(bf16)
    send(qs.at[:, 0:cut], qr.at[:, 0:cut], pair_send.at[1], pair_recv.at[1], partner)
    qs[:, cut:] = jnp.dot(theirs, weight_b, preferred_element_type=f32).astype(bf16)
    rest = pl.ds(cut, qs.shape[1] - cut)
    send(qs.at[:, rest], qr.at[:, rest], pair_send.at[3], pair_recv.at[3], partner)
    pump(2)
    ours = xn[yl]
    got_a = jnp.dot(ours, weight_a, preferred_element_type=f32)
    got_b = jnp.dot(ours, weight_b, preferred_element_type=f32)
    got = jnp.concatenate([got_a, got_b], axis=1)
    pump(2)
    arrived(ssr, pair_recv.at[0])
    square = (ssb[yl] + ssr[...]) * (1.0 / (2 * tile_blocks * width))
    inverse = lax.rsqrt(square[:, :1] + RMS_EPS)
    arrived(qr.at[:, 0:cut], pair_recv.at[1])
    arrived(qr.at[:, rest], pair_recv.at[3])
    pump(1)
    got = (got + qr[...].astype(f32)) * inverse
    heads = wq.shape[1] // size

    def rotated(v):
        return (v * cosine + pltpu.roll(v, size // 2, 1) * sine).astype(bf16).astype(f32)

    for h in range(heads):
        q = rotated(got[:, h * size:(h + 1) * size])
        for s in range(2):
            q3[:, s * heads + h, :] = q[s * rows:(s + 1) * rows]
    k_new = rotated(got[:, heads * size:(heads + 1) * size])
    v_new = got[:, (heads + 1) * size:(heads + 2) * size].astype(bf16).astype(f32)
    pump(2)

    key_load.wait()
    value_load.wait()
    scale = size ** -0.5
    slots = kc.shape[1]
    lane = lax.broadcasted_iota(jnp.int32, (CHUNK, 2 * heads, slots), 2).astype(f32)
    step_of = lax.broadcasted_iota(jnp.int32, (CHUNK, 2 * heads, 1), 1)
    for r0 in range(0, rows, CHUNK):
        pump(2)
        part = slice(r0, r0 + CHUNK)
        q = q3[part]
        scores = lax.dot_general(
            q.astype(bf16), kc[part], (((2,), (2,)), ((0,), (0,))), preferred_element_type=f32
        ) * scale
        live = live_rows[part][:, None, :]
        scores = jnp.where(lane < live, scores, -jnp.inf)
        k0, k1 = k_new[r0:r0 + CHUNK][:, None, :], k_new[rows + r0:rows + r0 + CHUNK][:, None, :]
        v0, v1 = v_new[r0:r0 + CHUNK][:, None, :], v_new[rows + r0:rows + r0 + CHUNK][:, None, :]
        n0 = jnp.sum(q * k0, axis=2, keepdims=True) * scale
        n1 = jnp.sum(q * k1, axis=2, keepdims=True) * scale
        n1 = jnp.where(step_of >= heads, n1, -jnp.inf)
        top = jnp.maximum(jnp.max(scores, axis=2, keepdims=True), jnp.maximum(n0, n1))
        probs = jnp.exp(scores - top)
        e0, e1 = jnp.exp(n0 - top), jnp.exp(n1 - top)
        total = jnp.sum(probs, axis=2, keepdims=True) + e0 + e1
        mixed = lax.dot_general(
            probs.astype(bf16), vc[part], (((2,), (1,)), ((0,), (0,))), preferred_element_type=f32
        )
        mixed = mixed + e0.astype(bf16).astype(f32) * v0 + e1.astype(bf16).astype(f32) * v1
        att3[part] = mixed / total
    attended = jnp.concatenate(
        [
            jnp.concatenate([att3[:, s * heads + h, :] for h in range(heads)], axis=1)
            for s in range(2)
        ],
        axis=0,
    ).astype(bf16)
    order = one_hot_rows(
        (2, NZ, 2, NX), lambda r_, z_, s_, x_: s_ * rows + r_ * half + z_ * NX + x_
    )
    attb[yl] = pick(order, attended).astype(bf16)
    send(attb.at[yl], attb.at[yl], pair_send.at[2], pair_recv.at[2], partner)

    pump(len(out_steps))
    stream_end(oa, ob, 1)
    arrived(attb.at[1 - yl], pair_recv.at[2])
    full = attb[...].reshape(2 * both, heads * size)
    tiles = NYH // 2
    slab = NZ // tile_blocks

    def project(j):
        left = oa[pl.ds(j * slab, slab)].reshape(width, ocut)
        right = ob[pl.ds(j * slab, slab)].reshape(width, ob.shape[2])
        dims = (((1,), (1,)), ((), ()))
        return lax.dot_general(
            full[:, :ocut], left, dims, preferred_element_type=f32
        ) + lax.dot_general(full[:, ocut:], right, dims, preferred_element_type=f32)

    for i in range(tiles):
        ps[i] = project(2 * i + 1 - c).astype(bf16)
        send(ps.at[i], pr.at[i], core_send.at[i], core_recv.at[i], sib)
    def at(yy):
        yy = lax.rem(yy + ny, ny)
        return dev(x, z, lax.rem(yy, 2), yy // 2, c)

    def ahead(m):
        return lax.rem(NYH * yl + m - y + 2 * ny, ny)

    cuts = [pl.ds(0, split), pl.ds(split, width - split)]

    def either(delta, *values):
        hit = delta == values[0]
        for value in values[1:]:
            hit = jnp.logical_or(hit, delta == value)
        return hit

    def far_copy(m, h, to):
        return remote(sp.at[m, :, cuts[h]], fb.at[m, :, cuts[h]], y_send.at[m, h], f_recv.at[m, h], to)

    def near_copy(m, h, side, to):
        return remote(sp.at[m, :, cuts[h]], rb.at[side, :, cuts[h]], y_send.at[m, h], y_recv.at[side, h], to)

    for i in range(tiles):
        kept = project(2 * i + c)
        arrived(pr.at[i], core_recv.at[i])
        summed = (kept + pr[i].astype(f32)).astype(bf16)
        for r in range(2):
            for g in range(2):
                lo = g * both + r * rows
                sp[2 * i + r, g * rows:(g + 1) * rows, :] = summed[lo:lo + rows]
        for h in range(2):
            for m in (2 * i, 2 * i + 1):
                delta = ahead(m)
                pl.when(either(delta, 3, 4) if h == 0 else delta == 3)(far_copy(m, h, at(y + 2)).start)
                pl.when(delta == 5 if h == 0 else either(delta, 4, 5))(far_copy(m, h, at(y - 2)).start)
                if h == 0:
                    pl.when(delta == 6)(near_copy(m, h, 1, at(NYH * yl + m)).start)
                else:
                    pl.when(delta == 2)(near_copy(m, h, 0, at(NYH * yl + m)).start)
    for h in range(2):
        lanes = slice(0, split) if h == 0 else slice(split, width)
        for m in range(NYH):
            delta = ahead(m)

            @pl.when(either(delta, 1, 7, 2 if h == 0 else 6))
            def _():
                arrived(fb.at[m, :, cuts[h]], f_recv.at[m, h])
                sp[m, :, lanes] = (sp[m, :, lanes].astype(f32) + fb[m, :, lanes].astype(f32)).astype(bf16)

            pl.when(either(delta, 1, 2) if h == 0 else delta == 1)(near_copy(m, h, 0, at(NYH * yl + m)).start)
            pl.when(delta == 7 if h == 0 else either(delta, 6, 7))(near_copy(m, h, 1, at(NYH * yl + m)).start)

    holds = jnp.where(y // NYH == yl, 1.0, 0.0)
    for h in range(2):
        lanes = slice(0, split) if h == 0 else slice(split, width)
        result = rr[:, :, lanes].reshape(both, -1).astype(f32)
        result = result + sp[lax.rem(y, NYH), :, lanes].astype(f32) * holds
        for side in range(2):
            arrived(rb.at[side, :, cuts[h]], y_recv.at[side, h])
            result = result + rb[side, :, lanes].astype(f32)
        result = result.reshape(2, NZ, 2 * NX, result.shape[1])
        for k in range(NZ):
            zs[k, :, lanes] = jnp.concatenate([result[0, k], result[1, k]], axis=0).astype(bf16)
        zr[z, :, lanes] = zs[z, :, lanes]
        for d in range(1, NZ):
            zz = lax.rem(z + d, NZ)
            send(zs.at[zz, :, cuts[h]], zr.at[z, :, cuts[h]], za_send.at[h, d - 1], za_recv.at[h, d - 1],
                 dev(x, zz, yl, yh, c))
    order = one_hot_rows(
        (NX, 2, NZ, 2), lambda x_, g_, z_, s_: ((z_ * 2 + g_) * 2 + s_) * NX + x_
    )
    for h in range(2):
        lanes = slice(0, split) if h == 0 else slice(split, width)
        for d in range(1, NZ):
            arrived(zr.at[lax.rem(z + NZ - d, NZ), :, cuts[h]], za_recv.at[h, d - 1])
        moved = pick(order, zr[:, :, lanes].reshape(both, -1)).astype(bf16)
        xo[:, :, lanes] = moved.reshape(NX, 4 * NZ, moved.shape[1])
        xr[x, :, lanes] = xo[x, :, lanes]
        for d in range(1, NX):
            xx = lax.rem(x + d, NX)
            send(xo.at[xx, :, cuts[h]], xr.at[x, :, cuts[h]], xa_send.at[h, d - 1], xa_recv.at[h, d - 1],
                 dev(xx, z, yl, yh, c))
    order = one_hot_rows(
        (2, NZ, NX, 2), lambda g_, z_, x_, s_: ((x_ * 2 + g_) * NZ + z_) * 2 + s_
    )
    for h in range(2):
        lanes = slice(0, split) if h == 0 else slice(split, width)
        for d in range(1, NX):
            arrived(xr.at[lax.rem(x + NX - d, NX), :, cuts[h]], xa_recv.at[h, d - 1])
        out[:, lanes] = pick(order, xr[:, :, lanes].reshape(both, -1)).astype(bf16)

    for copy in sent:
        copy.wait_send()
    for s, buf in ((0, wb), (1, ob)):
        for d in range(1, NX):
            view = buf.at[:, mine]
            remote(view, view, bx_send.at[s, d - 1], bx_recv.at[s, d - 1], sib).wait_send()
    for k in range(NYH):
        is_self = jnp.logical_and(yl_to == yl, yh == k)
        away = remote(xs, xg.at[yl, tile_me], xs_send.at[k], xs_recv.at[src_me], sib)
        pl.when(jnp.logical_not(is_self))(away.wait_send)
        for h in range(2):
            pl.when(ahead(k) != 0)(far_copy(k, h, sib).wait_send)


def on_device(
    hidden, next_hidden, gain, w_query, w_key, w_value, w_out,
    key_cache, value_cache, lengths, positions,
):
    rows, width = hidden.shape
    both = 2 * rows
    slots, size = key_cache.shape[2], key_cache.shape[3]
    block, qcols = w_query.shape
    heads = qcols // size
    columns = qcols + 2 * size
    cut, ocut = columns // 2, qcols // 2
    half_width = NYH * width

    tall = gain.reshape(-1, min(128, width))
    place = np.arange(size) % (size // 2)
    freqs = (ROPE_BASE ** (-(2.0 * place) / size)).astype(np.float32)[None, :]

    vmem = pl.BlockSpec(memory_space=pltpu.VMEM)
    hbm = pl.BlockSpec(memory_space=pl.ANY)
    dma = lambda *shape: pltpu.SemaphoreType.DMA(shape)
    steps = NZ // 2
    result = pl.pallas_call(
        layer_kernel,
        out_shape=jax.ShapeDtypeStruct((both, width), bf16),
        in_specs=[vmem] * 10 + [hbm] * 2,
        out_specs=vmem,
        scratch_shapes=[
            pltpu.VMEM((NZ, NX * block, cut), bf16),
            pltpu.VMEM((NZ, NX * block, columns - cut), bf16),
            pltpu.VMEM((NZ, NX * block, ocut), bf16),
            pltpu.VMEM((NZ, NX * block, qcols - ocut), bf16),
            pltpu.VMEM((both, width), bf16),
            pltpu.VMEM((2, NYH, both, width), bf16),
            pltpu.VMEM((2, both, half_width), bf16),
            pltpu.VMEM(tall.shape, f32),
            pltpu.VMEM((2, both, 128), f32),
            pltpu.VMEM((both, 128), f32),
            pltpu.VMEM((both, columns), bf16),
            pltpu.VMEM((both, columns), bf16),
            pltpu.VMEM((rows, slots, size), bf16),
            pltpu.VMEM((rows, slots, size), bf16),
            pltpu.VMEM((rows, 2 * heads, size), f32),
            pltpu.VMEM((rows, 2 * heads, size), f32),
            pltpu.VMEM((2, both, qcols), bf16),
            pltpu.VMEM((NYH // 2, 2 * both, width), bf16),
            pltpu.VMEM((NYH // 2, 2 * both, width), bf16),
            pltpu.VMEM((NYH, both, width), bf16),
            pltpu.VMEM((NYH, both, width), bf16),
            pltpu.VMEM((2, both, width), bf16),
            pltpu.VMEM((2, rows, width), bf16),
            pltpu.VMEM((NZ, 4 * NX, width), bf16),
            pltpu.VMEM((NZ, 4 * NX, width), bf16),
            pltpu.VMEM((NX, 4 * NZ, width), bf16),
            pltpu.VMEM((NX, 4 * NZ, width), bf16),
            dma(2),
            dma(NYH), dma(NYH), dma(NYH), dma(NYH), dma(2), dma(2),
            dma(2, NX - 1), dma(2, NX - 1), dma(2, 2, steps, NX), dma(2, 2, steps, NX),
            dma(2, NX - 1), dma(2, NX - 1), dma(2, 2, steps), dma(2, 2, steps),
            dma(4), dma(4), dma(NYH // 2), dma(NYH // 2), dma(NYH, 2), dma(NYH, 2), dma(2, 2),
            dma(2, NZ - 1), dma(2, NZ - 1), dma(2, NX - 1), dma(2, NX - 1),
        ],
        compiler_params=pltpu.CompilerParams(
            collective_id=0, has_side_effects=True, vmem_limit_bytes=56 * 1024 * 1024
        ),
        name="gathered_layer",
    )(
        hidden, next_hidden, tall, w_query, w_key, w_value, w_out.T,
        jnp.asarray(freqs), lengths[None, :], positions[None, :],
        key_cache.reshape(rows, slots, size), value_cache.reshape(rows, slots, size),
    )
    return result.reshape(rows, 2, 1, width)


def solution(mesh):
    placed = (
        P("fsdp", "tp"),
        P("fsdp", "tp"),
        P(),
        P("fsdp", "tp"),
        P("fsdp", "tp"),
        P("fsdp", "tp"),
        P("tp", "fsdp"),
        P("fsdp", "tp", None, None),
        P("fsdp", "tp", None, None),
        P("fsdp"),
        P("fsdp"),
    )
    return jax.shard_map(
        on_device,
        mesh=mesh,
        in_specs=placed,
        out_specs=P(None, None, "fsdp", "tp"),
        check_vma=False,
    )
```

```python
import functools

import jax
import jax.numpy as jnp
from jax import lax
from jax.experimental import pallas as pl
from jax.experimental.pallas import tpu as pltpu
from jax.sharding import PartitionSpec as P
import numpy as np

RMS_EPS = 1e-06
ROPE_BASE = 1000000.0
MESH = pl.DeviceIdType.MESH
NX, NZ, NYH = 4, 8, 4
CHUNK = 16

f32, bf16 = jnp.float32, jnp.bfloat16


def one_hot_rows(out_dims, source_of):
    count = 1
    for size in out_dims:
        count *= size
    row = lax.broadcasted_iota(jnp.int32, (count, count), 0)
    column = lax.broadcasted_iota(jnp.int32, (count, count), 1)
    digits, shift = [], 0
    for size in reversed(out_dims):
        bits = size.bit_length() - 1
        digits.append(lax.shift_right_logical(row, shift) & (size - 1))
        shift += bits
    digits.reverse()
    return jnp.where(source_of(*digits) == column, 1.0, 0.0).astype(bf16)


def pick(matrix, rows):
    return jnp.dot(matrix, rows, preferred_element_type=f32)


def layer_kernel(
    hid, nxt, gain, wq, wk, wv, wot, freq_ref, len_ref, pos_ref, kc_hbm, vc_hbm,
    out,
    wa, wb, oa, ob, xs, xg, xn, wide, ssb, ssr, qs, qr, kc, vc, q3, att3, attb,
    ps, pr, sp, fb, rb, rr, zs, zr, xo, xr,
    cache_sem, xs_send, xr_send, xs_recv, sib_send, sib_recv, res_send, res_recv,
    ax_send, ax_recv, az_send, az_recv, bx_send, bx_recv, bz_send, bz_recv,
    pair_send, pair_recv, core_send, core_recv, y_send, f_recv, y_recv,
    za_send, za_recv, xa_send, xa_recv,
):
    rows = hid.shape[0]
    half = rows // 2
    both = 2 * rows
    width = hid.shape[1]
    block = wq.shape[0]
    tile_blocks = NYH
    split = width // 256 * 128 + 128 if width >= 256 else width // 2
    f, t = lax.axis_index("fsdp"), lax.axis_index("tp")
    x, z, yl = lax.rem(f, NX), lax.rem(f // NX, NZ), f // (NX * NZ)
    yh, c = t // 2, lax.rem(t, 2)

    def dev(x_, z_, yl_, yh_, c_):
        return ((yl_ * NZ + z_) * NX + x_, yh_ * 2 + c_)

    def remote(src, dst, send, recv, where):
        return pltpu.make_async_remote_copy(
            src_ref=src, dst_ref=dst, send_sem=send, recv_sem=recv,
            device_id=where, device_id_type=MESH,
        )

    def arrived(dst, sem):
        pltpu.make_async_copy(dst, dst, sem).wait()

    sent = []

    def send(*args):
        copy = remote(*args)
        copy.start()
        sent.append(copy)

    key_load = pltpu.make_async_copy(kc_hbm, kc, cache_sem.at[0])
    value_load = pltpu.make_async_copy(vc_hbm, vc, cache_sem.at[1])
    key_load.start()
    value_load.start()

    y = 2 * yh + yl
    ny = 2 * NYH
    sib = dev(x, z, yl, yh, 1 - c)
    partner = dev(x, z, 1 - yl, yh, c)
    places = [dev(lax.rem(x + d, NX), z, yl, yh, c) for d in range(1, NX)]
    places += [dev(x, lax.rem(z + d, NZ), yl, yh, c) for d in range(1, NZ)]
    for d in range(1, ny):
        yy = lax.rem(y + d, ny)
        places.append(dev(x, z, lax.rem(yy, 2), yy // 2, c))
    places.append(sib)
    barrier = pltpu.get_barrier_semaphore()
    for where in places:
        pl.semaphore_signal(barrier, inc=1, device_id=where, device_id_type=MESH)

    mine = pl.ds(pl.multiple_of(x * block, block), block)
    cut = wa.shape[2]
    own = jnp.concatenate([wq[...], wk[...], wv[...]], axis=1)
    wa[z, mine, :] = own[:, :cut]
    wb[z, mine, :] = own[:, cut:]
    ocut = oa.shape[2]
    oa[z, mine, :] = wot[:, :ocut]
    ob[z, mine, :] = wot[:, ocut:]
    xs[0:rows, :] = hid[...]
    xs[rows:both, :] = nxt[...]
    pl.semaphore_wait(barrier, len(places))

    def at(yy):
        yy = lax.rem(yy + ny, ny)
        return dev(x, z, lax.rem(yy, 2), yy // 2, c)

    def either(delta, *values):
        hit = delta == values[0]
        for value in values[1:]:
            hit = jnp.logical_or(hit, delta == value)
        return hit

    halves = (pl.ds(0, rows), pl.ds(rows, rows))
    parity = y // NYH
    tile_me = lax.rem(yh, NYH // 2) * 2 + c
    src_me = lax.rem(y, NYH)

    def input_slot(m, h):
        return xg.at[m % 2, (m // 2) * 2 + c, halves[h]]

    def input_away(k, h):
        return remote(xs.at[halves[h]], xg.at[yl, tile_me, halves[h]],
                      xs_send.at[k, h], xs_recv.at[src_me, h], at(2 * k + parity))

    for k in range(NYH):
        delta = lax.rem(2 * k + parity - y + ny, ny)
        for h in range(2):
            here = pltpu.make_async_copy(
                xs.at[halves[h]], xg.at[yl, tile_me, halves[h]], xs_recv.at[src_me, h])
            pl.when(either(delta, 1, 2, 6, 7))(input_away(k, h).start)
            pl.when(delta == 0)(here.start)

    def input_relay(m, h, to):
        return remote(input_slot(m, h), input_slot(m, h), xr_send.at[m, h], xs_recv.at[m, h], to)

    def relays(m, h):
        delta = lax.rem(y - NYH * yl - m + 2 * ny, ny)
        onward = either(delta, 1, 2) if h == 0 else delta == 1
        back = delta == 7 if h == 0 else either(delta, 6, 7)
        return onward, back

    def to_sibling(m, h):
        return remote(input_slot(m, h), input_slot(m, h), sib_send.at[m, h], sib_recv.at[m, h], sib)

    def relay_inputs():
        for m in range(NYH):
            for h in range(2):
                onward, back = relays(m, h)

                @pl.when(jnp.logical_or(onward, back))
                def _():
                    arrived(input_slot(m, h), xs_recv.at[m, h])
                    to_sibling(m, h).start()

                pl.when(onward)(input_relay(m, h, at(y + 2)).start)
                pl.when(back)(input_relay(m, h, at(y - 2)).start)

    def end_inputs():
        for m in range(NYH):
            for h in range(2):
                onward, back = relays(m, h)

                @pl.when(jnp.logical_not(jnp.logical_or(onward, back)))
                def _():
                    arrived(input_slot(m, h), xs_recv.at[m, h])
                    to_sibling(m, h).start()

        for m in range(NYH):
            for h in range(2):
                arrived(xg.at[m % 2, (m // 2) * 2 + 1 - c, halves[h]], sib_recv.at[m, h])

    up = dev(x, lax.rem(z + 1, NZ), yl, yh, c)
    down = dev(x, lax.rem(z + NZ - 1, NZ), yl, yh, c)
    last = NZ // 2 - 1

    turns = tuple(range(NX)) if NX < 4 else (0, 1, 3, 2)

    def column(e):
        return pl.ds(pl.multiple_of(lax.rem(x + e, NX) * block, block), block)

    def plane(o):
        return lax.rem(z + NZ + o, NZ)

    def first_x(buf, s):
        for d in range(1, NX):
            there = dev(lax.rem(x + d, NX), z, yl, yh, c)
            send(buf.at[z, mine], buf.at[z, mine], ax_send.at[s, d - 1], ax_recv.at[s, d - 1], there)

    def carried(k, w, i):
        return k < last or (i < NX // 2) == (w == 0)

    def a_send(buf, s, k, i):
        for w, (to, zz) in enumerate(((up, plane(-k)), (down, plane(k)))):
            if carried(k, w, i):
                view = buf.at[zz, column(turns[i])]
                send(view, view, az_send.at[s, w, k, i], az_recv.at[s, w, k, i], to)

    def a_wait(buf, s, k, i):
        for w, zz in enumerate((plane(-1 - k), plane(1 + k))):
            if carried(k, w, i):
                arrived(buf.at[zz, column(turns[i])], az_recv.at[s, w, k, i])

    def b_send(buf, s, k):
        for w, (to, zz) in enumerate(((up, plane(-k)), (down, plane(k)))):
            if k < last or w == 0:
                send(buf.at[zz, mine], buf.at[zz, mine], bz_send.at[s, w, k], bz_recv.at[s, w, k], to)

    def b_wait(buf, s, k):
        for w, zz in enumerate((plane(-1 - k), plane(1 + k))):
            if k < last or w == 0:
                arrived(buf.at[zz, mine], bz_recv.at[s, w, k])

    def b_spread(buf, s, offsets):
        for o in offsets:
            for d in range(1, NX):
                there = dev(lax.rem(x + d, NX), z, yl, yh, c)
                view = buf.at[plane(o), mine]
                remote(view, view, bx_send.at[s, d - 1], bx_recv.at[s, d - 1], there).start()

    def wait_spread(buf, s):
        for d in range(1, NX):
            arrived(buf.at[:, column(NX - d)], bx_recv.at[s, d - 1])

    def stream(a_buf, b_buf, s):
        def start():
            a_send(a_buf, s, 0, 0)
            b_send(b_buf, s, 0)
            first_x(a_buf, s)
            b_spread(b_buf, s, (0,))

        def from_x(i):
            arrived(a_buf.at[z, column(turns[i])], ax_recv.at[s, NX - turns[i] - 1])
            a_send(a_buf, s, 0, i)

        def b_step(k):
            b_wait(b_buf, s, k)
            if k < last:
                b_send(b_buf, s, k + 1)
            b_spread(b_buf, s, (-1 - k,) if k == last else (-1 - k, 1 + k))

        def a_step(k, i):
            a_wait(a_buf, s, k, i)
            a_send(a_buf, s, k + 1, i)

        firsts = [functools.partial(from_x, i) for i in range(1, NX)]
        smalls = [functools.partial(b_step, k) for k in range(last + 1)]
        larges = [functools.partial(a_step, k, i) for k in range(last) for i in range(NX)]
        steps = [start] + firsts[:1] + smalls[:1] + firsts[1:]
        for small in smalls[1:]:
            steps += larges[:2] + [small]
            larges = larges[2:]
        steps += larges
        return steps

    def stream_end(a_buf, b_buf, s):
        for i in range(NX):
            a_wait(a_buf, s, last, i)
        wait_spread(b_buf, s)

    out_steps = stream(oa, ob, 1)

    def pump(count):
        for _ in range(min(count, len(out_steps))):
            out_steps.pop(0)()

    in_steps = stream(wa, wb, 0)
    in_steps.pop(0)()

    away_rows = half * (1 - yl)
    own_rows = half * yl
    for s in range(2):
        src = xs.at[pl.ds(pl.multiple_of(s * rows + away_rows, half), half)]
        send(src, rr.at[yl, pl.ds(s * half, half)], res_send.at[s], res_recv.at[s], partner)
        rr[yl, s * half:(s + 1) * half, :] = xs[pl.ds(pl.multiple_of(s * rows + own_rows, half), half), :]

    def as_column(row):
        grid = (rows, rows)
        diagonal = lax.broadcasted_iota(jnp.int32, grid, 0) == lax.broadcasted_iota(jnp.int32, grid, 1)
        spread = jnp.broadcast_to(row[...].astype(f32), grid)
        return jnp.sum(jnp.where(diagonal, spread, 0.0), axis=1, keepdims=True)

    size = kc.shape[2]
    for number, step in enumerate(in_steps):
        if number == 2 * NX:
            relay_inputs()
        step()

    pump(1)
    end_inputs()

    wide[...] = gain[...].astype(f32)
    piece = min(128, width)
    for g in range(2):
        total = jnp.zeros((both, 1), f32)
        for j in range(tile_blocks):
            values = xg[g, j].astype(f32)
            total = total + jnp.sum(values * values, axis=1, keepdims=True)
            for p in range(width // piece):
                row = (yl * tile_blocks + j) * (width // piece) + p
                xn[g, :, j * width + p * piece:j * width + (p + 1) * piece] = (
                    values[:, p * piece:(p + 1) * piece] * wide[pl.ds(row, 1), :]
                ).astype(bf16)
        ssb[g] = jnp.broadcast_to(total, (both, 128))
    send(ssb.at[1 - yl], ssr, pair_send.at[0], pair_recv.at[0], partner)
    pump(2)

    first_at = as_column(pos_ref)
    angle = jnp.concatenate([first_at, first_at + 1.0], axis=0) * freq_ref[...]
    lane = lax.broadcasted_iota(jnp.int32, (both, size), 1)
    cosine = jnp.cos(angle)
    sine = jnp.where(lane < size // 2, -1.0, 1.0) * jnp.sin(angle)
    live_rows = jnp.broadcast_to(as_column(len_ref), (rows, kc.shape[1]))

    for s in range(2):
        arrived(rr.at[1 - yl, pl.ds(s * half, half)], res_recv.at[s])
    order = one_hot_rows((NZ, 2, NX), lambda z_, s_, x_: s_ * half + z_ * NX + x_)
    for g in range(2):
        rr[g] = pick(order, rr[g]).astype(bf16)

    pump(1)
    stream_end(wa, wb, 0)
    depth = NZ * NX * block
    weight_a = wa[...].reshape(depth, cut)
    weight_b = wb[...].reshape(depth, wb.shape[2])
    theirs = xn[1 - yl]
    qs[:, :cut] = jnp.dot(theirs, weight_a, preferred_element_type=f32).astype(bf16)
    send(qs.at[:, 0:cut], qr.at[:, 0:cut], pair_send.at[1], pair_recv.at[1], partner)
    qs[:, cut:] = jnp.dot(theirs, weight_b, preferred_element_type=f32).astype(bf16)
    rest = pl.ds(cut, qs.shape[1] - cut)
    send(qs.at[:, rest], qr.at[:, rest], pair_send.at[3], pair_recv.at[3], partner)
    pump(2)
    ours = xn[yl]
    got_a = jnp.dot(ours, weight_a, preferred_element_type=f32)
    got_b = jnp.dot(ours, weight_b, preferred_element_type=f32)
    got = jnp.concatenate([got_a, got_b], axis=1)
    pump(2)
    arrived(ssr, pair_recv.at[0])
    square = (ssb[yl] + ssr[...]) * (1.0 / (2 * tile_blocks * width))
    inverse = lax.rsqrt(square[:, :1] + RMS_EPS)
    arrived(qr.at[:, 0:cut], pair_recv.at[1])
    arrived(qr.at[:, rest], pair_recv.at[3])
    pump(1)
    got = (got + qr[...].astype(f32)) * inverse
    heads = wq.shape[1] // size

    def rotated(v):
        return (v * cosine + pltpu.roll(v, size // 2, 1) * sine).astype(bf16).astype(f32)

    for h in range(heads):
        q = rotated(got[:, h * size:(h + 1) * size])
        for s in range(2):
            q3[:, s * heads + h, :] = q[s * rows:(s + 1) * rows]
    k_new = rotated(got[:, heads * size:(heads + 1) * size])
    v_new = got[:, (heads + 1) * size:(heads + 2) * size].astype(bf16).astype(f32)
    pump(2)

    key_load.wait()
    value_load.wait()
    scale = size ** -0.5
    slots = kc.shape[1]
    lane = lax.broadcasted_iota(jnp.int32, (CHUNK, 2 * heads, slots), 2).astype(f32)
    step_of = lax.broadcasted_iota(jnp.int32, (CHUNK, 2 * heads, 1), 1)
    for r0 in range(0, rows, CHUNK):
        pump(2)
        part = slice(r0, r0 + CHUNK)
        q = q3[part]
        scores = lax.dot_general(
            q.astype(bf16), kc[part], (((2,), (2,)), ((0,), (0,))), preferred_element_type=f32
        ) * scale
        live = live_rows[part][:, None, :]
        scores = jnp.where(lane < live, scores, -jnp.inf)
        k0, k1 = k_new[r0:r0 + CHUNK][:, None, :], k_new[rows + r0:rows + r0 + CHUNK][:, None, :]
        v0, v1 = v_new[r0:r0 + CHUNK][:, None, :], v_new[rows + r0:rows + r0 + CHUNK][:, None, :]
        n0 = jnp.sum(q * k0, axis=2, keepdims=True) * scale
        n1 = jnp.sum(q * k1, axis=2, keepdims=True) * scale
        n1 = jnp.where(step_of >= heads, n1, -jnp.inf)
        top = jnp.maximum(jnp.max(scores, axis=2, keepdims=True), jnp.maximum(n0, n1))
        probs = jnp.exp(scores - top)
        e0, e1 = jnp.exp(n0 - top), jnp.exp(n1 - top)
        total = jnp.sum(probs, axis=2, keepdims=True) + e0 + e1
        mixed = lax.dot_general(
            probs.astype(bf16), vc[part], (((2,), (1,)), ((0,), (0,))), preferred_element_type=f32
        )
        mixed = mixed + e0.astype(bf16).astype(f32) * v0 + e1.astype(bf16).astype(f32) * v1
        att3[part] = mixed / total
    attended = jnp.concatenate(
        [
            jnp.concatenate([att3[:, s * heads + h, :] for h in range(heads)], axis=1)
            for s in range(2)
        ],
        axis=0,
    ).astype(bf16)
    order = one_hot_rows(
        (2, NZ, 2, NX), lambda r_, z_, s_, x_: s_ * rows + r_ * half + z_ * NX + x_
    )
    attb[yl] = pick(order, attended).astype(bf16)
    send(attb.at[yl], attb.at[yl], pair_send.at[2], pair_recv.at[2], partner)

    pump(len(out_steps))
    stream_end(oa, ob, 1)
    arrived(attb.at[1 - yl], pair_recv.at[2])
    full = attb[...].reshape(2 * both, heads * size)
    tiles = NYH // 2
    slab = NZ // tile_blocks

    def project(j):
        left = oa[pl.ds(j * slab, slab)].reshape(width, ocut)
        right = ob[pl.ds(j * slab, slab)].reshape(width, ob.shape[2])
        dims = (((1,), (1,)), ((), ()))
        return lax.dot_general(
            full[:, :ocut], left, dims, preferred_element_type=f32
        ) + lax.dot_general(full[:, ocut:], right, dims, preferred_element_type=f32)

    for i in range(tiles):
        ps[i] = project(2 * i + 1 - c).astype(bf16)
        send(ps.at[i], pr.at[i], core_send.at[i], core_recv.at[i], sib)
    def ahead(m):
        return lax.rem(NYH * yl + m - y + 2 * ny, ny)

    cuts = [pl.ds(0, split), pl.ds(split, width - split)]

    def far_copy(m, h, to):
        return remote(sp.at[m, :, cuts[h]], fb.at[m, :, cuts[h]], y_send.at[m, h], f_recv.at[m, h], to)

    def near_copy(m, h, side, to):
        return remote(sp.at[m, :, cuts[h]], rb.at[side, :, cuts[h]], y_send.at[m, h], y_recv.at[side, h], to)

    for i in range(tiles):
        kept = project(2 * i + c)
        arrived(pr.at[i], core_recv.at[i])
        summed = (kept + pr[i].astype(f32)).astype(bf16)
        for r in range(2):
            for g in range(2):
                lo = g * both + r * rows
                sp[2 * i + r, g * rows:(g + 1) * rows, :] = summed[lo:lo + rows]
        for h in range(2):
            for m in (2 * i, 2 * i + 1):
                delta = ahead(m)
                pl.when(either(delta, 3, 4) if h == 0 else delta == 3)(far_copy(m, h, at(y + 2)).start)
                pl.when(delta == 5 if h == 0 else either(delta, 4, 5))(far_copy(m, h, at(y - 2)).start)
                if h == 0:
                    pl.when(delta == 6)(near_copy(m, h, 1, at(NYH * yl + m)).start)
                else:
                    pl.when(delta == 2)(near_copy(m, h, 0, at(NYH * yl + m)).start)
    for h in range(2):
        lanes = slice(0, split) if h == 0 else slice(split, width)
        for m in range(NYH):
            delta = ahead(m)

            @pl.when(either(delta, 1, 7, 2 if h == 0 else 6))
            def _():
                arrived(fb.at[m, :, cuts[h]], f_recv.at[m, h])
                sp[m, :, lanes] = (sp[m, :, lanes].astype(f32) + fb[m, :, lanes].astype(f32)).astype(bf16)

            pl.when(either(delta, 1, 2) if h == 0 else delta == 1)(near_copy(m, h, 0, at(NYH * yl + m)).start)
            pl.when(delta == 7 if h == 0 else either(delta, 6, 7))(near_copy(m, h, 1, at(NYH * yl + m)).start)

    holds = jnp.where(y // NYH == yl, 1.0, 0.0)
    for h in range(2):
        lanes = slice(0, split) if h == 0 else slice(split, width)
        result = rr[:, :, lanes].reshape(both, -1).astype(f32)
        result = result + sp[lax.rem(y, NYH), :, lanes].astype(f32) * holds
        for side in range(2):
            arrived(rb.at[side, :, cuts[h]], y_recv.at[side, h])
            result = result + rb[side, :, lanes].astype(f32)
        result = result.reshape(2, NZ, 2 * NX, result.shape[1])
        for k in range(NZ):
            zs[k, :, lanes] = jnp.concatenate([result[0, k], result[1, k]], axis=0).astype(bf16)
        zr[z, :, lanes] = zs[z, :, lanes]
        for d in range(1, NZ):
            zz = lax.rem(z + d, NZ)
            send(zs.at[zz, :, cuts[h]], zr.at[z, :, cuts[h]], za_send.at[h, d - 1], za_recv.at[h, d - 1],
                 dev(x, zz, yl, yh, c))
    order = one_hot_rows(
        (NX, 2, NZ, 2), lambda x_, g_, z_, s_: ((z_ * 2 + g_) * 2 + s_) * NX + x_
    )
    for h in range(2):
        lanes = slice(0, split) if h == 0 else slice(split, width)
        for d in range(1, NZ):
            arrived(zr.at[lax.rem(z + NZ - d, NZ), :, cuts[h]], za_recv.at[h, d - 1])
        moved = pick(order, zr[:, :, lanes].reshape(both, -1)).astype(bf16)
        xo[:, :, lanes] = moved.reshape(NX, 4 * NZ, moved.shape[1])
        xr[x, :, lanes] = xo[x, :, lanes]
        for d in range(1, NX):
            xx = lax.rem(x + d, NX)
            send(xo.at[xx, :, cuts[h]], xr.at[x, :, cuts[h]], xa_send.at[h, d - 1], xa_recv.at[h, d - 1],
                 dev(xx, z, yl, yh, c))
    order = one_hot_rows(
        (2, NZ, NX, 2), lambda g_, z_, x_, s_: ((x_ * 2 + g_) * NZ + z_) * 2 + s_
    )
    for h in range(2):
        lanes = slice(0, split) if h == 0 else slice(split, width)
        for d in range(1, NX):
            arrived(xr.at[lax.rem(x + NX - d, NX), :, cuts[h]], xa_recv.at[h, d - 1])
        out[:, lanes] = pick(order, xr[:, :, lanes].reshape(both, -1)).astype(bf16)

    for copy in sent:
        copy.wait_send()
    for s, buf in ((0, wb), (1, ob)):
        for d in range(1, NX):
            view = buf.at[:, mine]
            remote(view, view, bx_send.at[s, d - 1], bx_recv.at[s, d - 1], sib).wait_send()
    for k in range(NYH):
        for h in range(2):
            delta = lax.rem(2 * k + parity - y + ny, ny)
            pl.when(either(delta, 1, 2, 6, 7))(input_away(k, h).wait_send)
            pl.when(jnp.logical_or(*relays(k, h)))(input_relay(k, h, sib).wait_send)
            to_sibling(k, h).wait_send()
        for h in range(2):
            pl.when(ahead(k) != 0)(far_copy(k, h, sib).wait_send)


def on_device(
    hidden, next_hidden, gain, w_query, w_key, w_value, w_out,
    key_cache, value_cache, lengths, positions,
):
    rows, width = hidden.shape
    both = 2 * rows
    slots, size = key_cache.shape[2], key_cache.shape[3]
    block, qcols = w_query.shape
    heads = qcols // size
    columns = qcols + 2 * size
    cut, ocut = columns // 2, qcols // 2
    half_width = NYH * width

    tall = gain.reshape(-1, min(128, width))
    place = np.arange(size) % (size // 2)
    freqs = (ROPE_BASE ** (-(2.0 * place) / size)).astype(np.float32)[None, :]

    vmem = pl.BlockSpec(memory_space=pltpu.VMEM)
    hbm = pl.BlockSpec(memory_space=pl.ANY)
    dma = lambda *shape: pltpu.SemaphoreType.DMA(shape)
    steps = NZ // 2
    result = pl.pallas_call(
        layer_kernel,
        out_shape=jax.ShapeDtypeStruct((both, width), bf16),
        in_specs=[vmem] * 10 + [hbm] * 2,
        out_specs=vmem,
        scratch_shapes=[
            pltpu.VMEM((NZ, NX * block, cut), bf16),
            pltpu.VMEM((NZ, NX * block, columns - cut), bf16),
            pltpu.VMEM((NZ, NX * block, ocut), bf16),
            pltpu.VMEM((NZ, NX * block, qcols - ocut), bf16),
            pltpu.VMEM((both, width), bf16),
            pltpu.VMEM((2, NYH, both, width), bf16),
            pltpu.VMEM((2, both, half_width), bf16),
            pltpu.VMEM(tall.shape, f32),
            pltpu.VMEM((2, both, 128), f32),
            pltpu.VMEM((both, 128), f32),
            pltpu.VMEM((both, columns), bf16),
            pltpu.VMEM((both, columns), bf16),
            pltpu.VMEM((rows, slots, size), bf16),
            pltpu.VMEM((rows, slots, size), bf16),
            pltpu.VMEM((rows, 2 * heads, size), f32),
            pltpu.VMEM((rows, 2 * heads, size), f32),
            pltpu.VMEM((2, both, qcols), bf16),
            pltpu.VMEM((NYH // 2, 2 * both, width), bf16),
            pltpu.VMEM((NYH // 2, 2 * both, width), bf16),
            pltpu.VMEM((NYH, both, width), bf16),
            pltpu.VMEM((NYH, both, width), bf16),
            pltpu.VMEM((2, both, width), bf16),
            pltpu.VMEM((2, rows, width), bf16),
            pltpu.VMEM((NZ, 4 * NX, width), bf16),
            pltpu.VMEM((NZ, 4 * NX, width), bf16),
            pltpu.VMEM((NX, 4 * NZ, width), bf16),
            pltpu.VMEM((NX, 4 * NZ, width), bf16),
            dma(2),
            dma(NYH, 2), dma(NYH, 2), dma(NYH, 2), dma(NYH, 2), dma(NYH, 2), dma(2), dma(2),
            dma(2, NX - 1), dma(2, NX - 1), dma(2, 2, steps, NX), dma(2, 2, steps, NX),
            dma(2, NX - 1), dma(2, NX - 1), dma(2, 2, steps), dma(2, 2, steps),
            dma(4), dma(4), dma(NYH // 2), dma(NYH // 2), dma(NYH, 2), dma(NYH, 2), dma(2, 2),
            dma(2, NZ - 1), dma(2, NZ - 1), dma(2, NX - 1), dma(2, NX - 1),
        ],
        compiler_params=pltpu.CompilerParams(
            collective_id=0, has_side_effects=True, vmem_limit_bytes=56 * 1024 * 1024
        ),
        name="gathered_layer",
    )(
        hidden, next_hidden, tall, w_query, w_key, w_value, w_out.T,
        jnp.asarray(freqs), lengths[None, :], positions[None, :],
        key_cache.reshape(rows, slots, size), value_cache.reshape(rows, slots, size),
    )
    return result.reshape(rows, 2, 1, width)


def solution(mesh):
    placed = (
        P("fsdp", "tp"),
        P("fsdp", "tp"),
        P(),
        P("fsdp", "tp"),
        P("fsdp", "tp"),
        P("fsdp", "tp"),
        P("tp", "fsdp"),
        P("fsdp", "tp", None, None),
        P("fsdp", "tp", None, None),
        P("fsdp"),
        P("fsdp"),
    )
    return jax.shard_map(
        on_device,
        mesh=mesh,
        in_specs=placed,
        out_specs=P(None, None, "fsdp", "tp"),
        check_vma=False,
    )
```

```python
import functools

import jax
import jax.numpy as jnp
from jax import lax
from jax.experimental import pallas as pl
from jax.experimental.pallas import tpu as pltpu
from jax.sharding import PartitionSpec as P
import numpy as np

RMS_EPS = 1e-06
ROPE_BASE = 1000000.0
MESH = pl.DeviceIdType.MESH
NX, NZ, NYH = 4, 8, 4
CHUNK = 16

f32, bf16 = jnp.float32, jnp.bfloat16


def one_hot_rows(out_dims, source_of):
    count = 1
    for size in out_dims:
        count *= size
    row = lax.broadcasted_iota(jnp.int32, (count, count), 0)
    column = lax.broadcasted_iota(jnp.int32, (count, count), 1)
    digits, shift = [], 0
    for size in reversed(out_dims):
        bits = size.bit_length() - 1
        digits.append(lax.shift_right_logical(row, shift) & (size - 1))
        shift += bits
    digits.reverse()
    return jnp.where(source_of(*digits) == column, 1.0, 0.0).astype(bf16)


def pick(matrix, rows):
    return jnp.dot(matrix, rows, preferred_element_type=f32)


def layer_kernel(
    hid, nxt, gain, wq, wk, wv, wot, freq_ref, len_ref, pos_ref, kc_hbm, vc_hbm,
    out,
    wa, wb, oa, ob, xs, xg, xn, wide, ssb, ssr, qs, qr, kc, vc, q3, att3, attb,
    ps, pr, sp, fb, rb, rr, zs, zr, xo, xr,
    cache_sem, xs_send, xs_recv, sib_send, sib_recv, res_send, res_recv,
    ax_send, ax_recv, az_send, az_recv, bx_send, bx_recv, bz_send, bz_recv,
    pair_send, pair_recv, core_send, core_recv, y_send, f_recv, y_recv,
    za_send, za_recv, xa_send, xa_recv,
):
    rows = hid.shape[0]
    half = rows // 2
    both = 2 * rows
    width = hid.shape[1]
    block = wq.shape[0]
    tile_blocks = NYH
    split = width // 256 * 128 + 128 if width >= 256 else width // 2
    f, t = lax.axis_index("fsdp"), lax.axis_index("tp")
    x, z, yl = lax.rem(f, NX), lax.rem(f // NX, NZ), f // (NX * NZ)
    yh, c = t // 2, lax.rem(t, 2)

    def dev(x_, z_, yl_, yh_, c_):
        return ((yl_ * NZ + z_) * NX + x_, yh_ * 2 + c_)

    def remote(src, dst, send, recv, where):
        return pltpu.make_async_remote_copy(
            src_ref=src, dst_ref=dst, send_sem=send, recv_sem=recv,
            device_id=where, device_id_type=MESH,
        )

    def arrived(dst, sem):
        pltpu.make_async_copy(dst, dst, sem).wait()

    sent = []

    def send(*args):
        copy = remote(*args)
        copy.start()
        sent.append(copy)

    key_load = pltpu.make_async_copy(kc_hbm, kc, cache_sem.at[0])
    value_load = pltpu.make_async_copy(vc_hbm, vc, cache_sem.at[1])
    key_load.start()
    value_load.start()

    y = 2 * yh + yl
    ny = 2 * NYH
    sib = dev(x, z, yl, yh, 1 - c)
    partner = dev(x, z, 1 - yl, yh, c)
    places = [dev(lax.rem(x + d, NX), z, yl, yh, c) for d in range(1, NX)]
    places += [dev(x, lax.rem(z + d, NZ), yl, yh, c) for d in range(1, NZ)]
    for d in range(1, ny):
        yy = lax.rem(y + d, ny)
        places.append(dev(x, z, lax.rem(yy, 2), yy // 2, c))
    places.append(sib)
    barrier = pltpu.get_barrier_semaphore()
    for where in places:
        pl.semaphore_signal(barrier, inc=1, device_id=where, device_id_type=MESH)

    mine = pl.ds(pl.multiple_of(x * block, block), block)
    cut = wa.shape[2]
    own = jnp.concatenate([wq[...], wk[...], wv[...]], axis=1)
    wa[z, mine, :] = own[:, :cut]
    wb[z, mine, :] = own[:, cut:]
    ocut = oa.shape[2]
    oa[z, mine, :] = wot[:, :ocut]
    ob[z, mine, :] = wot[:, ocut:]
    xs[0:rows, :] = hid[...]
    xs[rows:both, :] = nxt[...]
    pl.semaphore_wait(barrier, len(places))

    yl_to = yh // (NYH // 2)
    tile_me = lax.rem(yh, NYH // 2) * 2 + c
    src_me = yl * (NYH // 2) + lax.rem(yh, NYH // 2)
    for k in range(NYH):
        is_self = jnp.logical_and(yl_to == yl, yh == k)
        there = dev(x, z, yl_to, k, c)
        away = remote(xs, xg.at[yl, tile_me], xs_send.at[k], xs_recv.at[src_me], there)
        here = pltpu.make_async_copy(xs, xg.at[yl, tile_me], xs_recv.at[src_me])
        pl.when(jnp.logical_not(is_self))(away.start)
        pl.when(is_self)(here.start)

    up = dev(x, lax.rem(z + 1, NZ), yl, yh, c)
    down = dev(x, lax.rem(z + NZ - 1, NZ), yl, yh, c)
    last = NZ // 2 - 1

    turns = tuple(range(NX)) if NX < 4 else (0, 1, 3, 2)

    def column(e):
        return pl.ds(pl.multiple_of(lax.rem(x + e, NX) * block, block), block)

    def plane(o):
        return lax.rem(z + NZ + o, NZ)

    def first_x(buf, s):
        for d in range(1, NX):
            there = dev(lax.rem(x + d, NX), z, yl, yh, c)
            send(buf.at[z, mine], buf.at[z, mine], ax_send.at[s, d - 1], ax_recv.at[s, d - 1], there)

    def carried(k, w, i):
        return k < last or (i < NX // 2) == (w == 0)

    def a_send(buf, s, k, i):
        for w, (to, zz) in enumerate(((up, plane(-k)), (down, plane(k)))):
            if carried(k, w, i):
                view = buf.at[zz, column(turns[i])]
                send(view, view, az_send.at[s, w, k, i], az_recv.at[s, w, k, i], to)

    def a_wait(buf, s, k, i):
        for w, zz in enumerate((plane(-1 - k), plane(1 + k))):
            if carried(k, w, i):
                arrived(buf.at[zz, column(turns[i])], az_recv.at[s, w, k, i])

    def b_send(buf, s, k):
        for w, (to, zz) in enumerate(((up, plane(-k)), (down, plane(k)))):
            if k < last or w == 0:
                send(buf.at[zz, mine], buf.at[zz, mine], bz_send.at[s, w, k], bz_recv.at[s, w, k], to)

    def b_wait(buf, s, k):
        for w, zz in enumerate((plane(-1 - k), plane(1 + k))):
            if k < last or w == 0:
                arrived(buf.at[zz, mine], bz_recv.at[s, w, k])

    def b_spread(buf, s, offsets):
        for o in offsets:
            for d in range(1, NX):
                there = dev(lax.rem(x + d, NX), z, yl, yh, c)
                view = buf.at[plane(o), mine]
                side = plane(o) // (NZ // 2)
                remote(view, view, bx_send.at[s, d - 1], bx_recv.at[s, d - 1, side], there).start()

    def wait_spread(buf, s, side):
        for d in range(1, NX):
            planes = pl.ds(pl.multiple_of(side * (NZ // 2), NZ // 2), NZ // 2)
            arrived(buf.at[planes, column(NX - d)], bx_recv.at[s, d - 1, side])

    def stream(a_buf, b_buf, s):
        def start():
            a_send(a_buf, s, 0, 0)
            b_send(b_buf, s, 0)
            first_x(a_buf, s)
            b_spread(b_buf, s, (0,))

        def from_x(i):
            arrived(a_buf.at[z, column(turns[i])], ax_recv.at[s, NX - turns[i] - 1])
            a_send(a_buf, s, 0, i)

        def b_step(k):
            b_wait(b_buf, s, k)
            if k < last:
                b_send(b_buf, s, k + 1)
            b_spread(b_buf, s, (-1 - k,) if k == last else (-1 - k, 1 + k))

        def a_step(k, i):
            a_wait(a_buf, s, k, i)
            a_send(a_buf, s, k + 1, i)

        steps = [start]
        steps += [functools.partial(from_x, i) for i in range(1, NX)]
        for k in range(last + 1):
            steps.append(functools.partial(b_step, k))
            if k < last:
                steps += [functools.partial(a_step, k, i) for i in range(NX)]
        return steps

    def last_blocks(a_buf, s):
        for i in range(NX):
            a_wait(a_buf, s, last, i)

    out_steps = stream(oa, ob, 1)

    def pump(count):
        for _ in range(min(count, len(out_steps))):
            out_steps.pop(0)()

    in_steps = stream(wa, wb, 0)
    in_steps.pop(0)()

    away_rows = half * (1 - yl)
    own_rows = half * yl
    for s in range(2):
        src = xs.at[pl.ds(pl.multiple_of(s * rows + away_rows, half), half)]
        send(src, rr.at[yl, pl.ds(s * half, half)], res_send.at[s], res_recv.at[s], partner)
        rr[yl, s * half:(s + 1) * half, :] = xs[pl.ds(pl.multiple_of(s * rows + own_rows, half), half), :]

    def as_column(row):
        grid = (rows, rows)
        diagonal = lax.broadcasted_iota(jnp.int32, grid, 0) == lax.broadcasted_iota(jnp.int32, grid, 1)
        spread = jnp.broadcast_to(row[...].astype(f32), grid)
        return jnp.sum(jnp.where(diagonal, spread, 0.0), axis=1, keepdims=True)

    size = kc.shape[2]
    for step in in_steps:
        step()

    for k in range(NYH):
        slot = xg.at[k // (NYH // 2), (k % (NYH // 2)) * 2 + c]
        arrived(slot, xs_recv.at[k])
        send(slot, slot, sib_send.at[k], sib_recv.at[k], sib)
    pump(1)
    for k in range(NYH):
        arrived(xg.at[k // (NYH // 2), (k % (NYH // 2)) * 2 + (1 - c)], sib_recv.at[k])

    wide[...] = gain[...].astype(f32)
    piece = min(128, width)
    for g in range(2):
        total = jnp.zeros((both, 1), f32)
        for j in range(tile_blocks):
            values = xg[g, j].astype(f32)
            total = total + jnp.sum(values * values, axis=1, keepdims=True)
            for p in range(width // piece):
                row = (yl * tile_blocks + j) * (width // piece) + p
                xn[g, :, j * width + p * piece:j * width + (p + 1) * piece] = (
                    values[:, p * piece:(p + 1) * piece] * wide[pl.ds(row, 1), :]
                ).astype(bf16)
        ssb[g] = jnp.broadcast_to(total, (both, 128))
    send(ssb.at[1 - yl], ssr, pair_send.at[0], pair_recv.at[0], partner)
    pump(2)

    first_at = as_column(pos_ref)
    angle = jnp.concatenate([first_at, first_at + 1.0], axis=0) * freq_ref[...]
    lane = lax.broadcasted_iota(jnp.int32, (both, size), 1)
    cosine = jnp.cos(angle)
    sine = jnp.where(lane < size // 2, -1.0, 1.0) * jnp.sin(angle)
    live_rows = jnp.broadcast_to(as_column(len_ref), (rows, kc.shape[1]))

    for s in range(2):
        arrived(rr.at[1 - yl, pl.ds(s * half, half)], res_recv.at[s])
    order = one_hot_rows((NZ, 2, NX), lambda z_, s_, x_: s_ * half + z_ * NX + x_)
    for g in range(2):
        rr[g] = pick(order, rr[g]).astype(bf16)

    pump(1)
    wait_spread(wb, 0, 0)
    wait_spread(wb, 0, 1)
    depth = NZ * NX * block
    weight_b = wb[...].reshape(depth, wb.shape[2])
    theirs = xn[1 - yl]
    qs[:, cut:] = jnp.dot(theirs, weight_b, preferred_element_type=f32).astype(bf16)
    rest = pl.ds(cut, qs.shape[1] - cut)
    send(qs.at[:, rest], qr.at[:, rest], pair_send.at[3], pair_recv.at[3], partner)
    last_blocks(wa, 0)
    weight_a = wa[...].reshape(depth, cut)
    qs[:, :cut] = jnp.dot(theirs, weight_a, preferred_element_type=f32).astype(bf16)
    send(qs.at[:, 0:cut], qr.at[:, 0:cut], pair_send.at[1], pair_recv.at[1], partner)
    pump(2)
    ours = xn[yl]
    got_a = jnp.dot(ours, weight_a, preferred_element_type=f32)
    got_b = jnp.dot(ours, weight_b, preferred_element_type=f32)
    got = jnp.concatenate([got_a, got_b], axis=1)
    pump(2)
    arrived(ssr, pair_recv.at[0])
    square = (ssb[yl] + ssr[...]) * (1.0 / (2 * tile_blocks * width))
    inverse = lax.rsqrt(square[:, :1] + RMS_EPS)
    arrived(qr.at[:, 0:cut], pair_recv.at[1])
    arrived(qr.at[:, rest], pair_recv.at[3])
    pump(1)
    got = (got + qr[...].astype(f32)) * inverse
    heads = wq.shape[1] // size

    def rotated(v):
        return (v * cosine + pltpu.roll(v, size // 2, 1) * sine).astype(bf16).astype(f32)

    for h in range(heads):
        q = rotated(got[:, h * size:(h + 1) * size])
        for s in range(2):
            q3[:, s * heads + h, :] = q[s * rows:(s + 1) * rows]
    k_new = rotated(got[:, heads * size:(heads + 1) * size])
    v_new = got[:, (heads + 1) * size:(heads + 2) * size].astype(bf16).astype(f32)
    pump(2)

    key_load.wait()
    value_load.wait()
    scale = size ** -0.5
    slots = kc.shape[1]
    lane = lax.broadcasted_iota(jnp.int32, (CHUNK, 2 * heads, slots), 2).astype(f32)
    step_of = lax.broadcasted_iota(jnp.int32, (CHUNK, 2 * heads, 1), 1)
    for r0 in range(0, rows, CHUNK):
        pump(2)
        part = slice(r0, r0 + CHUNK)
        q = q3[part]
        scores = lax.dot_general(
            q.astype(bf16), kc[part], (((2,), (2,)), ((0,), (0,))), preferred_element_type=f32
        ) * scale
        live = live_rows[part][:, None, :]
        scores = jnp.where(lane < live, scores, -jnp.inf)
        k0, k1 = k_new[r0:r0 + CHUNK][:, None, :], k_new[rows + r0:rows + r0 + CHUNK][:, None, :]
        v0, v1 = v_new[r0:r0 + CHUNK][:, None, :], v_new[rows + r0:rows + r0 + CHUNK][:, None, :]
        n0 = jnp.sum(q * k0, axis=2, keepdims=True) * scale
        n1 = jnp.sum(q * k1, axis=2, keepdims=True) * scale
        n1 = jnp.where(step_of >= heads, n1, -jnp.inf)
        top = jnp.maximum(jnp.max(scores, axis=2, keepdims=True), jnp.maximum(n0, n1))
        probs = jnp.exp(scores - top)
        e0, e1 = jnp.exp(n0 - top), jnp.exp(n1 - top)
        total = jnp.sum(probs, axis=2, keepdims=True) + e0 + e1
        mixed = lax.dot_general(
            probs.astype(bf16), vc[part], (((2,), (1,)), ((0,), (0,))), preferred_element_type=f32
        )
        mixed = mixed + e0.astype(bf16).astype(f32) * v0 + e1.astype(bf16).astype(f32) * v1
        att3[part] = mixed / total
        if (r0 + CHUNK) % half == 0:
            lo = r0 + CHUNK - half
            attended = jnp.concatenate(
                [
                    jnp.concatenate([att3[lo:lo + half, s * heads + h, :] for h in range(heads)], axis=1)
                    for s in range(2)
                ],
                axis=0,
            ).astype(bf16)
            attb[yl, 2 * lo:2 * (lo + half), :] = pick(order, attended).astype(bf16)
            group = attb.at[yl, pl.ds(2 * lo, rows)]
            send(group, group, pair_send.at[4 + lo // half], pair_recv.at[4 + lo // half], partner)
    pump(len(out_steps))
    near = z // (NZ // 2)
    wait_spread(ob, 1, near)
    for r in range(2):
        arrived(attb.at[1 - yl, pl.ds(r * rows, rows)], pair_recv.at[4 + r])
    full = attb[...].reshape(2 * both, heads * size)
    tiles = NYH // 2
    slab = NZ // tile_blocks

    def project(j):
        left = oa[pl.ds(j * slab, slab)].reshape(width, ocut)
        right = ob[pl.ds(j * slab, slab)].reshape(width, ob.shape[2])
        dims = (((1,), (1,)), ((), ()))
        return lax.dot_general(
            full[:, :ocut], left, dims, preferred_element_type=f32
        ) + lax.dot_general(full[:, ocut:], right, dims, preferred_element_type=f32)

    def at(yy):
        yy = lax.rem(yy + ny, ny)
        return dev(x, z, lax.rem(yy, 2), yy // 2, c)

    def ahead(m):
        return lax.rem(NYH * yl + m - y + 2 * ny, ny)

    cuts = [pl.ds(0, split), pl.ds(split, width - split)]

    def either(delta, *values):
        hit = delta == values[0]
        for value in values[1:]:
            hit = jnp.logical_or(hit, delta == value)
        return hit

    def far_copy(m, h, to):
        return remote(sp.at[m, :, cuts[h]], fb.at[m, :, cuts[h]], y_send.at[m, h], f_recv.at[m, h], to)

    def near_copy(m, h, side, to):
        return remote(sp.at[m, :, cuts[h]], rb.at[side, :, cuts[h]], y_send.at[m, h], y_recv.at[side, h], to)

    half_tiles = (near, 1 - near)
    for n, i in enumerate(half_tiles):
        if n == 1:
            last_blocks(oa, 1)
            wait_spread(ob, 1, i)
        ps[i] = project(2 * i + 1 - c).astype(bf16)
        send(ps.at[i], pr.at[i], core_send.at[i], core_recv.at[i], sib)
        kept = project(2 * i + c)
        arrived(pr.at[i], core_recv.at[i])
        summed = (kept + pr[i].astype(f32)).astype(bf16)
        for r in range(2):
            for g in range(2):
                lo = g * both + r * rows
                sp[2 * i + r, g * rows:(g + 1) * rows, :] = summed[lo:lo + rows]
        for h in range(2):
            for m in (2 * i, 2 * i + 1):
                delta = ahead(m)
                pl.when(either(delta, 3, 4) if h == 0 else delta == 3)(far_copy(m, h, at(y + 2)).start)
                pl.when(delta == 5 if h == 0 else either(delta, 4, 5))(far_copy(m, h, at(y - 2)).start)
                if h == 0:
                    pl.when(delta == 6)(near_copy(m, h, 1, at(NYH * yl + m)).start)
                else:
                    pl.when(delta == 2)(near_copy(m, h, 0, at(NYH * yl + m)).start)
    for h in range(2):
        lanes = slice(0, split) if h == 0 else slice(split, width)
        for m in [2 * i + r for i in half_tiles for r in range(2)]:
            delta = ahead(m)

            @pl.when(either(delta, 1, 7, 2 if h == 0 else 6))
            def _():
                arrived(fb.at[m, :, cuts[h]], f_recv.at[m, h])
                sp[m, :, lanes] = (sp[m, :, lanes].astype(f32) + fb[m, :, lanes].astype(f32)).astype(bf16)

            pl.when(either(delta, 1, 2) if h == 0 else delta == 1)(near_copy(m, h, 0, at(NYH * yl + m)).start)
            pl.when(delta == 7 if h == 0 else either(delta, 6, 7))(near_copy(m, h, 1, at(NYH * yl + m)).start)

    holds = jnp.where(y // NYH == yl, 1.0, 0.0)
    for h in range(2):
        lanes = slice(0, split) if h == 0 else slice(split, width)
        result = rr[:, :, lanes].reshape(both, -1).astype(f32)
        result = result + sp[lax.rem(y, NYH), :, lanes].astype(f32) * holds
        for side in range(2):
            arrived(rb.at[side, :, cuts[h]], y_recv.at[side, h])
            result = result + rb[side, :, lanes].astype(f32)
        result = result.reshape(2, NZ, 2 * NX, result.shape[1])
        for k in range(NZ):
            zs[k, :, lanes] = jnp.concatenate([result[0, k], result[1, k]], axis=0).astype(bf16)
        zr[z, :, lanes] = zs[z, :, lanes]
        for d in range(1, NZ):
            zz = lax.rem(z + d, NZ)
            send(zs.at[zz, :, cuts[h]], zr.at[z, :, cuts[h]], za_send.at[h, d - 1], za_recv.at[h, d - 1],
                 dev(x, zz, yl, yh, c))
    order = one_hot_rows(
        (NX, 2, NZ, 2), lambda x_, g_, z_, s_: ((z_ * 2 + g_) * 2 + s_) * NX + x_
    )
    for h in range(2):
        lanes = slice(0, split) if h == 0 else slice(split, width)
        for d in range(1, NZ):
            arrived(zr.at[lax.rem(z + NZ - d, NZ), :, cuts[h]], za_recv.at[h, d - 1])
        moved = pick(order, zr[:, :, lanes].reshape(both, -1)).astype(bf16)
        xo[:, :, lanes] = moved.reshape(NX, 4 * NZ, moved.shape[1])
        xr[x, :, lanes] = xo[x, :, lanes]
        for d in range(1, NX):
            xx = lax.rem(x + d, NX)
            send(xo.at[xx, :, cuts[h]], xr.at[x, :, cuts[h]], xa_send.at[h, d - 1], xa_recv.at[h, d - 1],
                 dev(xx, z, yl, yh, c))
    order = one_hot_rows(
        (2, NZ, NX, 2), lambda g_, z_, x_, s_: ((x_ * 2 + g_) * NZ + z_) * 2 + s_
    )
    for h in range(2):
        lanes = slice(0, split) if h == 0 else slice(split, width)
        for d in range(1, NX):
            arrived(xr.at[lax.rem(x + NX - d, NX), :, cuts[h]], xa_recv.at[h, d - 1])
        out[:, lanes] = pick(order, xr[:, :, lanes].reshape(both, -1)).astype(bf16)

    for copy in sent:
        copy.wait_send()
    for s, buf in ((0, wb), (1, ob)):
        for d in range(1, NX):
            view = buf.at[:, mine]
            remote(view, view, bx_send.at[s, d - 1], bx_recv.at[s, d - 1, 0], sib).wait_send()
    for k in range(NYH):
        is_self = jnp.logical_and(yl_to == yl, yh == k)
        away = remote(xs, xg.at[yl, tile_me], xs_send.at[k], xs_recv.at[src_me], sib)
        pl.when(jnp.logical_not(is_self))(away.wait_send)
        for h in range(2):
            pl.when(ahead(k) != 0)(far_copy(k, h, sib).wait_send)


def on_device(
    hidden, next_hidden, gain, w_query, w_key, w_value, w_out,
    key_cache, value_cache, lengths, positions,
):
    rows, width = hidden.shape
    both = 2 * rows
    slots, size = key_cache.shape[2], key_cache.shape[3]
    block, qcols = w_query.shape
    heads = qcols // size
    columns = qcols + 2 * size
    cut, ocut = columns // 2, qcols // 2
    half_width = NYH * width

    tall = gain.reshape(-1, min(128, width))
    place = np.arange(size) % (size // 2)
    freqs = (ROPE_BASE ** (-(2.0 * place) / size)).astype(np.float32)[None, :]

    vmem = pl.BlockSpec(memory_space=pltpu.VMEM)
    hbm = pl.BlockSpec(memory_space=pl.ANY)
    dma = lambda *shape: pltpu.SemaphoreType.DMA(shape)
    steps = NZ // 2
    result = pl.pallas_call(
        layer_kernel,
        out_shape=jax.ShapeDtypeStruct((both, width), bf16),
        in_specs=[vmem] * 10 + [hbm] * 2,
        out_specs=vmem,
        scratch_shapes=[
            pltpu.VMEM((NZ, NX * block, cut), bf16),
            pltpu.VMEM((NZ, NX * block, columns - cut), bf16),
            pltpu.VMEM((NZ, NX * block, ocut), bf16),
            pltpu.VMEM((NZ, NX * block, qcols - ocut), bf16),
            pltpu.VMEM((both, width), bf16),
            pltpu.VMEM((2, NYH, both, width), bf16),
            pltpu.VMEM((2, both, half_width), bf16),
            pltpu.VMEM(tall.shape, f32),
            pltpu.VMEM((2, both, 128), f32),
            pltpu.VMEM((both, 128), f32),
            pltpu.VMEM((both, columns), bf16),
            pltpu.VMEM((both, columns), bf16),
            pltpu.VMEM((rows, slots, size), bf16),
            pltpu.VMEM((rows, slots, size), bf16),
            pltpu.VMEM((rows, 2 * heads, size), f32),
            pltpu.VMEM((rows, 2 * heads, size), f32),
            pltpu.VMEM((2, both, qcols), bf16),
            pltpu.VMEM((NYH // 2, 2 * both, width), bf16),
            pltpu.VMEM((NYH // 2, 2 * both, width), bf16),
            pltpu.VMEM((NYH, both, width), bf16),
            pltpu.VMEM((NYH, both, width), bf16),
            pltpu.VMEM((2, both, width), bf16),
            pltpu.VMEM((2, rows, width), bf16),
            pltpu.VMEM((NZ, 4 * NX, width), bf16),
            pltpu.VMEM((NZ, 4 * NX, width), bf16),
            pltpu.VMEM((NX, 4 * NZ, width), bf16),
            pltpu.VMEM((NX, 4 * NZ, width), bf16),
            dma(2),
            dma(NYH), dma(NYH), dma(NYH), dma(NYH), dma(2), dma(2),
            dma(2, NX - 1), dma(2, NX - 1), dma(2, 2, steps, NX), dma(2, 2, steps, NX),
            dma(2, NX - 1), dma(2, NX - 1, 2), dma(2, 2, steps), dma(2, 2, steps),
            dma(6), dma(6), dma(NYH // 2), dma(NYH // 2), dma(NYH, 2), dma(NYH, 2), dma(2, 2),
            dma(2, NZ - 1), dma(2, NZ - 1), dma(2, NX - 1), dma(2, NX - 1),
        ],
        compiler_params=pltpu.CompilerParams(
            collective_id=0, has_side_effects=True, vmem_limit_bytes=56 * 1024 * 1024
        ),
        name="gathered_layer",
    )(
        hidden, next_hidden, tall, w_query, w_key, w_value, w_out.T,
        jnp.asarray(freqs), lengths[None, :], positions[None, :],
        key_cache.reshape(rows, slots, size), value_cache.reshape(rows, slots, size),
    )
    return result.reshape(rows, 2, 1, width)


def solution(mesh):
    placed = (
        P("fsdp", "tp"),
        P("fsdp", "tp"),
        P(),
        P("fsdp", "tp"),
        P("fsdp", "tp"),
        P("fsdp", "tp"),
        P("tp", "fsdp"),
        P("fsdp", "tp", None, None),
        P("fsdp", "tp", None, None),
        P("fsdp"),
        P("fsdp"),
    )
    return jax.shard_map(
        on_device,
        mesh=mesh,
        in_specs=placed,
        out_specs=P(None, None, "fsdp", "tp"),
        check_vma=False,
    )
```

```python
import functools

import jax
import jax.numpy as jnp
from jax import lax
from jax.experimental import pallas as pl
from jax.experimental.pallas import tpu as pltpu
from jax.sharding import PartitionSpec as P
import numpy as np

RMS_EPS = 1e-06
ROPE_BASE = 1000000.0
MESH = pl.DeviceIdType.MESH
NX, NZ, NYH = 4, 8, 4
CHUNK = 16

f32, bf16 = jnp.float32, jnp.bfloat16


def one_hot_rows(out_dims, source_of):
    count = 1
    for size in out_dims:
        count *= size
    row = lax.broadcasted_iota(jnp.int32, (count, count), 0)
    column = lax.broadcasted_iota(jnp.int32, (count, count), 1)
    digits, shift = [], 0
    for size in reversed(out_dims):
        bits = size.bit_length() - 1
        digits.append(lax.shift_right_logical(row, shift) & (size - 1))
        shift += bits
    digits.reverse()
    return jnp.where(source_of(*digits) == column, 1.0, 0.0).astype(bf16)


def pick(matrix, rows):
    return jnp.dot(matrix, rows, preferred_element_type=f32)


def layer_kernel(
    hid, nxt, gain, wq, wk, wv, wot, freq_hbm, len_hbm, pos_hbm, kc_hbm, vc_hbm,
    out,
    freq_ref, len_ref, pos_ref, load_sem, wa, wb, oa, ob, xs, xg, xn, wide, ssb, ssr, qs, qr, kc, vc, q3, att3, attb,
    ps, pr, sp, fb, rb, rr, zs, zr, xo, xr,
    cache_sem, xs_send, xs_recv, sib_send, sib_recv, res_send, res_recv,
    ax_send, ax_recv, az_send, az_recv, bx_send, bx_recv, bz_send, bz_recv,
    pair_send, pair_recv, core_send, core_recv, y_send, f_recv, y_recv,
    za_send, za_recv, xa_send, xa_recv,
):
    rows = hid.shape[0]
    half = rows // 2
    both = 2 * rows
    width = hid.shape[1]
    block = wq.shape[0]
    tile_blocks = NYH
    split = width // 256 * 128 + 128 if width >= 256 else width // 2
    f, t = lax.axis_index("fsdp"), lax.axis_index("tp")
    x, z, yl = lax.rem(f, NX), lax.rem(f // NX, NZ), f // (NX * NZ)
    yh, c = t // 2, lax.rem(t, 2)

    def dev(x_, z_, yl_, yh_, c_):
        return ((yl_ * NZ + z_) * NX + x_, yh_ * 2 + c_)

    def remote(src, dst, send, recv, where):
        return pltpu.make_async_remote_copy(
            src_ref=src, dst_ref=dst, send_sem=send, recv_sem=recv,
            device_id=where, device_id_type=MESH,
        )

    def arrived(dst, sem):
        pltpu.make_async_copy(dst, dst, sem).wait()

    sent = []

    def send(*args):
        copy = remote(*args)
        copy.start()
        sent.append(copy)

    mine = pl.ds(pl.multiple_of(x * block, block), block)
    cut, ocut = wa.shape[2], oa.shape[2]
    qcols, size = wq.shape[1], kc.shape[2]
    loads = [
        (hid, xs.at[pl.ds(0, rows)]),
        (nxt, xs.at[pl.ds(rows, rows)]),
        (wq.at[:, pl.ds(0, cut)], wa.at[z, mine]),
        (wq.at[:, pl.ds(cut, qcols - cut)], wb.at[z, mine, pl.ds(0, qcols - cut)]),
        (wk, wb.at[z, mine, pl.ds(qcols - cut, size)]),
        (wv, wb.at[z, mine, pl.ds(qcols - cut + size, size)]),
        (wot.at[:, pl.ds(0, ocut)], oa.at[z, mine]),
        (wot.at[:, pl.ds(ocut, qcols - ocut)], ob.at[z, mine]),
        (freq_hbm, freq_ref), (len_hbm, len_ref), (pos_hbm, pos_ref),
    ]
    loads = [pltpu.make_async_copy(src, dst, load_sem.at[n]) for n, (src, dst) in enumerate(loads)]
    for load in loads:
        load.start()

    y = 2 * yh + yl
    ny = 2 * NYH
    sib = dev(x, z, yl, yh, 1 - c)
    partner = dev(x, z, 1 - yl, yh, c)
    places = [dev(lax.rem(x + d, NX), z, yl, yh, c) for d in range(1, NX)]
    places += [dev(x, lax.rem(z + d, NZ), yl, yh, c) for d in range(1, NZ)]
    for d in range(1, ny):
        yy = lax.rem(y + d, ny)
        places.append(dev(x, z, lax.rem(yy, 2), yy // 2, c))
    places.append(sib)
    barrier = pltpu.get_barrier_semaphore()
    for where in places:
        pl.semaphore_signal(barrier, inc=1, device_id=where, device_id_type=MESH)

    for load in loads:
        load.wait()
    pl.semaphore_wait(barrier, len(places))
    key_load = pltpu.make_async_copy(kc_hbm, kc, cache_sem.at[0])
    value_load = pltpu.make_async_copy(vc_hbm, vc, cache_sem.at[1])

    yl_to = yh // (NYH // 2)
    tile_me = lax.rem(yh, NYH // 2) * 2 + c
    src_me = yl * (NYH // 2) + lax.rem(yh, NYH // 2)
    for k in range(NYH):
        is_self = jnp.logical_and(yl_to == yl, yh == k)
        there = dev(x, z, yl_to, k, c)
        away = remote(xs, xg.at[yl, tile_me], xs_send.at[k], xs_recv.at[src_me], there)
        here = pltpu.make_async_copy(xs, xg.at[yl, tile_me], xs_recv.at[src_me])
        pl.when(jnp.logical_not(is_self))(away.start)
        pl.when(is_self)(here.start)

    up = dev(x, lax.rem(z + 1, NZ), yl, yh, c)
    down = dev(x, lax.rem(z + NZ - 1, NZ), yl, yh, c)
    last = NZ // 2 - 1

    turns = tuple(range(NX)) if NX < 4 else (0, 1, 3, 2)

    def column(e):
        return pl.ds(pl.multiple_of(lax.rem(x + e, NX) * block, block), block)

    def plane(o):
        return lax.rem(z + NZ + o, NZ)

    def first_x(buf, s):
        for d in range(1, NX):
            there = dev(lax.rem(x + d, NX), z, yl, yh, c)
            send(buf.at[z, mine], buf.at[z, mine], ax_send.at[s, d - 1], ax_recv.at[s, d - 1], there)

    def carried(k, w, i):
        return k < last or (i < NX // 2) == (w == 0)

    def a_send(buf, s, k, i):
        for w, (to, zz) in enumerate(((up, plane(-k)), (down, plane(k)))):
            if carried(k, w, i):
                view = buf.at[zz, column(turns[i])]
                send(view, view, az_send.at[s, w, k, i], az_recv.at[s, w, k, i], to)

    def a_wait(buf, s, k, i):
        for w, zz in enumerate((plane(-1 - k), plane(1 + k))):
            if carried(k, w, i):
                arrived(buf.at[zz, column(turns[i])], az_recv.at[s, w, k, i])

    def b_send(buf, s, k):
        for w, (to, zz) in enumerate(((up, plane(-k)), (down, plane(k)))):
            if k < last or w == 0:
                send(buf.at[zz, mine], buf.at[zz, mine], bz_send.at[s, w, k], bz_recv.at[s, w, k], to)

    def b_wait(buf, s, k):
        for w, zz in enumerate((plane(-1 - k), plane(1 + k))):
            if k < last or w == 0:
                arrived(buf.at[zz, mine], bz_recv.at[s, w, k])

    def b_spread(buf, s, offsets):
        for o in offsets:
            for d in range(1, NX):
                there = dev(lax.rem(x + d, NX), z, yl, yh, c)
                view = buf.at[plane(o), mine]
                side = plane(o) // (NZ // 2)
                remote(view, view, bx_send.at[s, d - 1], bx_recv.at[s, d - 1, side], there).start()

    def wait_spread(buf, s, side):
        for d in range(1, NX):
            planes = pl.ds(pl.multiple_of(side * (NZ // 2), NZ // 2), NZ // 2)
            arrived(buf.at[planes, column(NX - d)], bx_recv.at[s, d - 1, side])

    def stream(a_buf, b_buf, s):
        def start():
            a_send(a_buf, s, 0, 0)
            b_send(b_buf, s, 0)
            first_x(a_buf, s)
            b_spread(b_buf, s, (0,))

        def from_x(i):
            arrived(a_buf.at[z, column(turns[i])], ax_recv.at[s, NX - turns[i] - 1])
            a_send(a_buf, s, 0, i)

        def b_step(k):
            b_wait(b_buf, s, k)
            if k < last:
                b_send(b_buf, s, k + 1)
            b_spread(b_buf, s, (-1 - k,) if k == last else (-1 - k, 1 + k))

        def a_step(k, i):
            a_wait(a_buf, s, k, i)
            a_send(a_buf, s, k + 1, i)

        if s == 1:
            firsts = [functools.partial(from_x, i) for i in range(1, NX)]
            smalls = [functools.partial(b_step, k) for k in range(last + 1)]
            larges = [functools.partial(a_step, k, i) for k in range(last) for i in range(NX)]
            steps = [start] + firsts[:1] + smalls[:1] + firsts[1:]
            for small in smalls[1:]:
                steps += larges[:2] + [small]
                larges = larges[2:]
            return steps + larges
        steps = [start]
        steps += [functools.partial(from_x, i) for i in range(1, NX)]
        for k in range(last + 1):
            steps.append(functools.partial(b_step, k))
            if k < last:
                steps += [functools.partial(a_step, k, i) for i in range(NX)]
        return steps

    def last_blocks(a_buf, s):
        for i in range(NX):
            a_wait(a_buf, s, last, i)

    out_steps = stream(oa, ob, 1)

    def pump(count):
        for _ in range(min(count, len(out_steps))):
            out_steps.pop(0)()

    in_steps = stream(wa, wb, 0)
    in_steps.pop(0)()

    away_rows = half * (1 - yl)
    own_rows = half * yl
    for s in range(2):
        src = xs.at[pl.ds(pl.multiple_of(s * rows + away_rows, half), half)]
        send(src, rr.at[yl, pl.ds(s * half, half)], res_send.at[s], res_recv.at[s], partner)
        rr[yl, s * half:(s + 1) * half, :] = xs[pl.ds(pl.multiple_of(s * rows + own_rows, half), half), :]

    def as_column(row):
        grid = (rows, rows)
        diagonal = lax.broadcasted_iota(jnp.int32, grid, 0) == lax.broadcasted_iota(jnp.int32, grid, 1)
        spread = jnp.broadcast_to(row[...].astype(f32), grid)
        return jnp.sum(jnp.where(diagonal, spread, 0.0), axis=1, keepdims=True)

    size = kc.shape[2]
    for number, step in enumerate(in_steps):
        step()
        if number == 2 * len(in_steps) // 3:
            pump(1)

    for k in range(NYH):
        slot = xg.at[k // (NYH // 2), (k % (NYH // 2)) * 2 + c]
        arrived(slot, xs_recv.at[k])
        send(slot, slot, sib_send.at[k], sib_recv.at[k], sib)
    pump(3)
    for k in range(NYH):
        arrived(xg.at[k // (NYH // 2), (k % (NYH // 2)) * 2 + (1 - c)], sib_recv.at[k])

    wide[...] = gain[...].astype(f32)
    piece = min(128, width)
    for g in range(2):
        total = jnp.zeros((both, 1), f32)
        for j in range(tile_blocks):
            values = xg[g, j].astype(f32)
            total = total + jnp.sum(values * values, axis=1, keepdims=True)
            for p in range(width // piece):
                row = (yl * tile_blocks + j) * (width // piece) + p
                xn[g, :, j * width + p * piece:j * width + (p + 1) * piece] = (
                    values[:, p * piece:(p + 1) * piece] * wide[pl.ds(row, 1), :]
                ).astype(bf16)
        ssb[g] = jnp.broadcast_to(total, (both, 128))
    send(ssb.at[1 - yl], ssr, pair_send.at[0], pair_recv.at[0], partner)
    pump(2)

    key_load.start()
    value_load.start()
    first_at = as_column(pos_ref)
    angle = jnp.concatenate([first_at, first_at + 1.0], axis=0) * freq_ref[...]
    lane = lax.broadcasted_iota(jnp.int32, (both, size), 1)
    cosine = jnp.cos(angle)
    sine = jnp.where(lane < size // 2, -1.0, 1.0) * jnp.sin(angle)
    live_rows = jnp.broadcast_to(as_column(len_ref), (rows, kc.shape[1]))

    for s in range(2):
        arrived(rr.at[1 - yl, pl.ds(s * half, half)], res_recv.at[s])
    order = one_hot_rows((NZ, 2, NX), lambda z_, s_, x_: s_ * half + z_ * NX + x_)
    for g in range(2):
        rr[g] = pick(order, rr[g]).astype(bf16)

    pump(2)
    wait_spread(wb, 0, 0)
    wait_spread(wb, 0, 1)
    depth = NZ * NX * block
    weight_b = wb[...].reshape(depth, wb.shape[2])
    theirs = xn[1 - yl]
    qs[:, cut:] = jnp.dot(theirs, weight_b, preferred_element_type=f32).astype(bf16)
    rest = pl.ds(cut, qs.shape[1] - cut)
    send(qs.at[:, rest], qr.at[:, rest], pair_send.at[3], pair_recv.at[3], partner)
    last_blocks(wa, 0)
    weight_a = wa[...].reshape(depth, cut)
    qs[:, :cut] = jnp.dot(theirs, weight_a, preferred_element_type=f32).astype(bf16)
    send(qs.at[:, 0:cut], qr.at[:, 0:cut], pair_send.at[1], pair_recv.at[1], partner)
    pump(2)
    ours = xn[yl]
    got_a = jnp.dot(ours, weight_a, preferred_element_type=f32)
    got_b = jnp.dot(ours, weight_b, preferred_element_type=f32)
    got = jnp.concatenate([got_a, got_b], axis=1)
    pump(2)
    arrived(ssr, pair_recv.at[0])
    square = (ssb[yl] + ssr[...]) * (1.0 / (2 * tile_blocks * width))
    inverse = lax.rsqrt(square[:, :1] + RMS_EPS)
    arrived(qr.at[:, 0:cut], pair_recv.at[1])
    arrived(qr.at[:, rest], pair_recv.at[3])
    pump(2)
    got = (got + qr[...].astype(f32)) * inverse
    heads = qcols // size

    def rotated(v):
        return (v * cosine + pltpu.roll(v, size // 2, 1) * sine).astype(bf16).astype(f32)

    for h in range(heads):
        q = rotated(got[:, h * size:(h + 1) * size])
        for s in range(2):
            q3[:, s * heads + h, :] = q[s * rows:(s + 1) * rows]
    k_new = rotated(got[:, heads * size:(heads + 1) * size])
    v_new = got[:, (heads + 1) * size:(heads + 2) * size].astype(bf16).astype(f32)
    pump(2)

    key_load.wait()
    value_load.wait()
    scale = size ** -0.5
    slots = kc.shape[1]
    lane = lax.broadcasted_iota(jnp.int32, (CHUNK, 2 * heads, slots), 2).astype(f32)
    step_of = lax.broadcasted_iota(jnp.int32, (CHUNK, 2 * heads, 1), 1)
    for r0 in range(0, rows, CHUNK):
        pump(2)
        part = slice(r0, r0 + CHUNK)
        q = q3[part]
        scores = lax.dot_general(
            q.astype(bf16), kc[part], (((2,), (2,)), ((0,), (0,))), preferred_element_type=f32
        ) * scale
        live = live_rows[part][:, None, :]
        scores = jnp.where(lane < live, scores, -jnp.inf)
        k0, k1 = k_new[r0:r0 + CHUNK][:, None, :], k_new[rows + r0:rows + r0 + CHUNK][:, None, :]
        v0, v1 = v_new[r0:r0 + CHUNK][:, None, :], v_new[rows + r0:rows + r0 + CHUNK][:, None, :]
        n0 = jnp.sum(q * k0, axis=2, keepdims=True) * scale
        n1 = jnp.sum(q * k1, axis=2, keepdims=True) * scale
        n1 = jnp.where(step_of >= heads, n1, -jnp.inf)
        top = jnp.maximum(jnp.max(scores, axis=2, keepdims=True), jnp.maximum(n0, n1))
        probs = jnp.exp(scores - top)
        e0, e1 = jnp.exp(n0 - top), jnp.exp(n1 - top)
        total = jnp.sum(probs, axis=2, keepdims=True) + e0 + e1
        mixed = lax.dot_general(
            probs.astype(bf16), vc[part], (((2,), (1,)), ((0,), (0,))), preferred_element_type=f32
        )
        mixed = mixed + e0.astype(bf16).astype(f32) * v0 + e1.astype(bf16).astype(f32) * v1
        att3[part] = mixed / total
        if (r0 + CHUNK) % half == 0:
            lo = r0 + CHUNK - half
            attended = jnp.concatenate(
                [
                    jnp.concatenate([att3[lo:lo + half, s * heads + h, :] for h in range(heads)], axis=1)
                    for s in range(2)
                ],
                axis=0,
            ).astype(bf16)
            attb[yl, 2 * lo:2 * (lo + half), :] = pick(order, attended).astype(bf16)
            group = attb.at[yl, pl.ds(2 * lo, rows)]
            send(group, group, pair_send.at[4 + lo // half], pair_recv.at[4 + lo // half], partner)
    pump(len(out_steps))
    near = z // (NZ // 2)
    wait_spread(ob, 1, near)
    for r in range(2):
        arrived(attb.at[1 - yl, pl.ds(r * rows, rows)], pair_recv.at[4 + r])
    full = attb[...].reshape(2 * both, heads * size)
    tiles = NYH // 2
    slab = NZ // tile_blocks

    def project(j):
        left = oa[pl.ds(j * slab, slab)].reshape(width, ocut)
        right = ob[pl.ds(j * slab, slab)].reshape(width, ob.shape[2])
        dims = (((1,), (1,)), ((), ()))
        return lax.dot_general(
            full[:, :ocut], left, dims, preferred_element_type=f32
        ) + lax.dot_general(full[:, ocut:], right, dims, preferred_element_type=f32)

    def at(yy):
        yy = lax.rem(yy + ny, ny)
        return dev(x, z, lax.rem(yy, 2), yy // 2, c)

    def ahead(m):
        return lax.rem(NYH * yl + m - y + 2 * ny, ny)

    cuts = [pl.ds(0, split), pl.ds(split, width - split)]

    def either(delta, *values):
        hit = delta == values[0]
        for value in values[1:]:
            hit = jnp.logical_or(hit, delta == value)
        return hit

    def far_copy(m, h, to):
        return remote(sp.at[m, :, cuts[h]], fb.at[m, :, cuts[h]], y_send.at[m, h], f_recv.at[m, h], to)

    def near_copy(m, h, side, to):
        return remote(sp.at[m, :, cuts[h]], rb.at[side, :, cuts[h]], y_send.at[m, h], y_recv.at[side, h], to)

    half_tiles = (near, 1 - near)
    for n, i in enumerate(half_tiles):
        if n == 1:
            last_blocks(oa, 1)
            wait_spread(ob, 1, i)
        ps[i] = project(2 * i + 1 - c).astype(bf16)
        send(ps.at[i], pr.at[i], core_send.at[i], core_recv.at[i], sib)
        kept = project(2 * i + c)
        arrived(pr.at[i], core_recv.at[i])
        summed = (kept + pr[i].astype(f32)).astype(bf16)
        for r in range(2):
            for g in range(2):
                lo = g * both + r * rows
                sp[2 * i + r, g * rows:(g + 1) * rows, :] = summed[lo:lo + rows]
        for h in range(2):
            for m in (2 * i, 2 * i + 1):
                delta = ahead(m)
                pl.when(either(delta, 3, 4) if h == 0 else delta == 3)(far_copy(m, h, at(y + 2)).start)
                pl.when(delta == 5 if h == 0 else either(delta, 4, 5))(far_copy(m, h, at(y - 2)).start)
                if h == 0:
                    pl.when(delta == 6)(near_copy(m, h, 1, at(NYH * yl + m)).start)
                else:
                    pl.when(delta == 2)(near_copy(m, h, 0, at(NYH * yl + m)).start)
    for h in range(2):
        lanes = slice(0, split) if h == 0 else slice(split, width)
        for m in [2 * i + r for i in half_tiles for r in range(2)]:
            delta = ahead(m)

            @pl.when(either(delta, 1, 7, 2 if h == 0 else 6))
            def _():
                arrived(fb.at[m, :, cuts[h]], f_recv.at[m, h])
                sp[m, :, lanes] = (sp[m, :, lanes].astype(f32) + fb[m, :, lanes].astype(f32)).astype(bf16)

            pl.when(either(delta, 1, 2) if h == 0 else delta == 1)(near_copy(m, h, 0, at(NYH * yl + m)).start)
            pl.when(delta == 7 if h == 0 else either(delta, 6, 7))(near_copy(m, h, 1, at(NYH * yl + m)).start)

    holds = jnp.where(y // NYH == yl, 1.0, 0.0)
    for h in range(2):
        lanes = slice(0, split) if h == 0 else slice(split, width)
        result = rr[:, :, lanes].reshape(both, -1).astype(f32)
        result = result + sp[lax.rem(y, NYH), :, lanes].astype(f32) * holds
        for side in range(2):
            arrived(rb.at[side, :, cuts[h]], y_recv.at[side, h])
            result = result + rb[side, :, lanes].astype(f32)
        result = result.reshape(2, NZ, 2 * NX, result.shape[1])
        for k in range(NZ):
            zs[k, :, lanes] = jnp.concatenate([result[0, k], result[1, k]], axis=0).astype(bf16)
        zr[z, :, lanes] = zs[z, :, lanes]
        for d in range(1, NZ):
            zz = lax.rem(z + d, NZ)
            send(zs.at[zz, :, cuts[h]], zr.at[z, :, cuts[h]], za_send.at[h, d - 1], za_recv.at[h, d - 1],
                 dev(x, zz, yl, yh, c))
    order = one_hot_rows(
        (NX, 2, NZ, 2), lambda x_, g_, z_, s_: ((z_ * 2 + g_) * 2 + s_) * NX + x_
    )
    for h in range(2):
        lanes = slice(0, split) if h == 0 else slice(split, width)
        for d in range(1, NZ):
            arrived(zr.at[lax.rem(z + NZ - d, NZ), :, cuts[h]], za_recv.at[h, d - 1])
        moved = pick(order, zr[:, :, lanes].reshape(both, -1)).astype(bf16)
        xo[:, :, lanes] = moved.reshape(NX, 4 * NZ, moved.shape[1])
        xr[x, :, lanes] = xo[x, :, lanes]
        for d in range(1, NX):
            xx = lax.rem(x + d, NX)
            send(xo.at[xx, :, cuts[h]], xr.at[x, :, cuts[h]], xa_send.at[h, d - 1], xa_recv.at[h, d - 1],
                 dev(xx, z, yl, yh, c))
    order = one_hot_rows(
        (2, NZ, NX, 2), lambda g_, z_, x_, s_: ((x_ * 2 + g_) * NZ + z_) * 2 + s_
    )
    for h in range(2):
        lanes = slice(0, split) if h == 0 else slice(split, width)
        for d in range(1, NX):
            arrived(xr.at[lax.rem(x + NX - d, NX), :, cuts[h]], xa_recv.at[h, d - 1])
        out[:, lanes] = pick(order, xr[:, :, lanes].reshape(both, -1)).astype(bf16)

    for copy in sent:
        copy.wait_send()
    for s, buf in ((0, wb), (1, ob)):
        for d in range(1, NX):
            view = buf.at[:, mine]
            remote(view, view, bx_send.at[s, d - 1], bx_recv.at[s, d - 1, 0], sib).wait_send()
    for k in range(NYH):
        is_self = jnp.logical_and(yl_to == yl, yh == k)
        away = remote(xs, xg.at[yl, tile_me], xs_send.at[k], xs_recv.at[src_me], sib)
        pl.when(jnp.logical_not(is_self))(away.wait_send)
        for h in range(2):
            pl.when(ahead(k) != 0)(far_copy(k, h, sib).wait_send)


def on_device(
    hidden, next_hidden, gain, w_query, w_key, w_value, w_out,
    key_cache, value_cache, lengths, positions,
):
    rows, width = hidden.shape
    both = 2 * rows
    slots, size = key_cache.shape[2], key_cache.shape[3]
    block, qcols = w_query.shape
    heads = qcols // size
    columns = qcols + 2 * size
    cut, ocut = columns // 2, qcols // 2
    half_width = NYH * width

    tall = gain.reshape(-1, min(128, width))
    place = np.arange(size) % (size // 2)
    freqs = (ROPE_BASE ** (-(2.0 * place) / size)).astype(np.float32)[None, :]

    vmem = pl.BlockSpec(memory_space=pltpu.VMEM)
    hbm = pl.BlockSpec(memory_space=pl.ANY)
    dma = lambda *shape: pltpu.SemaphoreType.DMA(shape)
    steps = NZ // 2
    result = pl.pallas_call(
        layer_kernel,
        out_shape=jax.ShapeDtypeStruct((both, width), bf16),
        in_specs=[hbm] * 2 + [vmem] + [hbm] * 9,
        out_specs=vmem,
        scratch_shapes=[
            pltpu.VMEM((1, size), f32),
            pltpu.VMEM((1, rows), jnp.int32),
            pltpu.VMEM((1, rows), jnp.int32),
            dma(11),
            pltpu.VMEM((NZ, NX * block, cut), bf16),
            pltpu.VMEM((NZ, NX * block, columns - cut), bf16),
            pltpu.VMEM((NZ, NX * block, ocut), bf16),
            pltpu.VMEM((NZ, NX * block, qcols - ocut), bf16),
            pltpu.VMEM((both, width), bf16),
            pltpu.VMEM((2, NYH, both, width), bf16),
            pltpu.VMEM((2, both, half_width), bf16),
            pltpu.VMEM(tall.shape, f32),
            pltpu.VMEM((2, both, 128), f32),
            pltpu.VMEM((both, 128), f32),
            pltpu.VMEM((both, columns), bf16),
            pltpu.VMEM((both, columns), bf16),
            pltpu.VMEM((rows, slots, size), bf16),
            pltpu.VMEM((rows, slots, size), bf16),
            pltpu.VMEM((rows, 2 * heads, size), f32),
            pltpu.VMEM((rows, 2 * heads, size), f32),
            pltpu.VMEM((2, both, qcols), bf16),
            pltpu.VMEM((NYH // 2, 2 * both, width), bf16),
            pltpu.VMEM((NYH // 2, 2 * both, width), bf16),
            pltpu.VMEM((NYH, both, width), bf16),
            pltpu.VMEM((NYH, both, width), bf16),
            pltpu.VMEM((2, both, width), bf16),
            pltpu.VMEM((2, rows, width), bf16),
            pltpu.VMEM((NZ, 4 * NX, width), bf16),
            pltpu.VMEM((NZ, 4 * NX, width), bf16),
            pltpu.VMEM((NX, 4 * NZ, width), bf16),
            pltpu.VMEM((NX, 4 * NZ, width), bf16),
            dma(2),
            dma(NYH), dma(NYH), dma(NYH), dma(NYH), dma(2), dma(2),
            dma(2, NX - 1), dma(2, NX - 1), dma(2, 2, steps, NX), dma(2, 2, steps, NX),
            dma(2, NX - 1), dma(2, NX - 1, 2), dma(2, 2, steps), dma(2, 2, steps),
            dma(6), dma(6), dma(NYH // 2), dma(NYH // 2), dma(NYH, 2), dma(NYH, 2), dma(2, 2),
            dma(2, NZ - 1), dma(2, NZ - 1), dma(2, NX - 1), dma(2, NX - 1),
        ],
        compiler_params=pltpu.CompilerParams(
            collective_id=0, has_side_effects=True, vmem_limit_bytes=56 * 1024 * 1024
        ),
        name="gathered_layer",
    )(
        hidden, next_hidden, tall, w_query, w_key, w_value, w_out.T,
        jnp.asarray(freqs), lengths[None, :], positions[None, :],
        key_cache.reshape(rows, slots, size), value_cache.reshape(rows, slots, size),
    )
    return result.reshape(rows, 2, 1, width)


def solution(mesh):
    placed = (
        P("fsdp", "tp"),
        P("fsdp", "tp"),
        P(),
        P("fsdp", "tp"),
        P("fsdp", "tp"),
        P("fsdp", "tp"),
        P("tp", "fsdp"),
        P("fsdp", "tp", None, None),
        P("fsdp", "tp", None, None),
        P("fsdp"),
        P("fsdp"),
    )
    return jax.shard_map(
        on_device,
        mesh=mesh,
        in_specs=placed,
        out_specs=P(None, None, "fsdp", "tp"),
        check_vma=False,
    )
```

```python
import functools

import jax
import jax.numpy as jnp
from jax import lax
from jax.experimental import pallas as pl
from jax.experimental.pallas import tpu as pltpu
from jax.sharding import PartitionSpec as P
import numpy as np

RMS_EPS = 1e-06
ROPE_BASE = 1000000.0
MESH = pl.DeviceIdType.MESH
NX, NZ, NYH = 4, 8, 4
CHUNK = 16

f32, bf16 = jnp.float32, jnp.bfloat16


def one_hot_rows(out_dims, source_of):
    count = 1
    for size in out_dims:
        count *= size
    row = lax.broadcasted_iota(jnp.int32, (count, count), 0)
    column = lax.broadcasted_iota(jnp.int32, (count, count), 1)
    digits, shift = [], 0
    for size in reversed(out_dims):
        bits = size.bit_length() - 1
        digits.append(lax.shift_right_logical(row, shift) & (size - 1))
        shift += bits
    digits.reverse()
    return jnp.where(source_of(*digits) == column, 1.0, 0.0).astype(bf16)


def pick(matrix, rows):
    return jnp.dot(matrix, rows, preferred_element_type=f32)


def layer_kernel(
    hid, nxt, gain, wq, wk, wv, wot, freq_ref, len_ref, pos_ref, kc_hbm, vc_hbm,
    out,
    wa, wb, oa, ob, xs, xg, xn, wide, ssb, ssr, qs, qr, kc, vc, q3, att3, attb,
    ps, pr, sp, fb, rb, rr, zs, zr, xo, xr,
    cache_sem, xs_send, xs_recv, sib_send, sib_recv, res_send, res_recv,
    ax_send, ax_recv, az_send, az_recv, bx_send, bx_recv, bz_send, bz_recv,
    pair_send, pair_recv, core_send, core_recv, y_send, f_recv, y_recv,
    za_send, za_recv, xa_send, xa_recv,
):
    rows = hid.shape[0]
    half = rows // 2
    both = 2 * rows
    width = hid.shape[1]
    block = wq.shape[0]
    tile_blocks = NYH
    split = width // 256 * 128 + 128 if width >= 256 else width // 2
    f, t = lax.axis_index("fsdp"), lax.axis_index("tp")
    x, z, yl = lax.rem(f, NX), lax.rem(f // NX, NZ), f // (NX * NZ)
    yh, c = t // 2, lax.rem(t, 2)

    def dev(x_, z_, yl_, yh_, c_):
        return ((yl_ * NZ + z_) * NX + x_, yh_ * 2 + c_)

    def remote(src, dst, send, recv, where):
        return pltpu.make_async_remote_copy(
            src_ref=src, dst_ref=dst, send_sem=send, recv_sem=recv,
            device_id=where, device_id_type=MESH,
        )

    def arrived(dst, sem):
        pltpu.make_async_copy(dst, dst, sem).wait()

    sent = []

    def send(*args):
        copy = remote(*args)
        copy.start()
        sent.append(copy)

    key_load = pltpu.make_async_copy(kc_hbm, kc, cache_sem.at[0])
    value_load = pltpu.make_async_copy(vc_hbm, vc, cache_sem.at[1])
    key_load.start()
    value_load.start()

    y = 2 * yh + yl
    ny = 2 * NYH
    sib = dev(x, z, yl, yh, 1 - c)
    partner = dev(x, z, 1 - yl, yh, c)
    places = [dev(lax.rem(x + d, NX), z, yl, yh, c) for d in range(1, NX)]
    places += [dev(x, lax.rem(z + d, NZ), yl, yh, c) for d in range(1, NZ)]
    for d in range(1, ny):
        yy = lax.rem(y + d, ny)
        places.append(dev(x, z, lax.rem(yy, 2), yy // 2, c))
    places.append(sib)
    barrier = pltpu.get_barrier_semaphore()
    for where in places:
        pl.semaphore_signal(barrier, inc=1, device_id=where, device_id_type=MESH)

    mine = pl.ds(pl.multiple_of(x * block, block), block)
    cut = wa.shape[2]
    own = jnp.concatenate([wq[...], wk[...], wv[...]], axis=1)
    wa[z, mine, :] = own[:, :cut]
    wb[z, mine, :] = own[:, cut:]
    ocut = oa.shape[2]
    oa[z, mine, :] = wot[:, :ocut]
    ob[z, mine, :] = wot[:, ocut:]
    xs[0:rows, :] = hid[...]
    xs[rows:both, :] = nxt[...]
    pl.semaphore_wait(barrier, len(places))

    yl_to = yh // (NYH // 2)
    tile_me = lax.rem(yh, NYH // 2) * 2 + c
    src_me = yl * (NYH // 2) + lax.rem(yh, NYH // 2)
    for k in range(NYH):
        is_self = jnp.logical_and(yl_to == yl, yh == k)
        there = dev(x, z, yl_to, k, c)
        away = remote(xs, xg.at[yl, tile_me], xs_send.at[k], xs_recv.at[src_me], there)
        here = pltpu.make_async_copy(xs, xg.at[yl, tile_me], xs_recv.at[src_me])
        pl.when(jnp.logical_not(is_self))(away.start)
        pl.when(is_self)(here.start)

    up = dev(x, lax.rem(z + 1, NZ), yl, yh, c)
    down = dev(x, lax.rem(z + NZ - 1, NZ), yl, yh, c)
    last = NZ // 2 - 1

    turns = tuple(range(NX)) if NX < 4 else (0, 1, 3, 2)

    def column(e):
        return pl.ds(pl.multiple_of(lax.rem(x + e, NX) * block, block), block)

    def plane(o):
        return lax.rem(z + NZ + o, NZ)

    def first_x(buf, s):
        for d in range(1, NX):
            there = dev(lax.rem(x + d, NX), z, yl, yh, c)
            send(buf.at[z, mine], buf.at[z, mine], ax_send.at[s, d - 1], ax_recv.at[s, d - 1], there)

    def carried(k, w, i):
        return k < last or (i < NX // 2) == (w == 0)

    def a_send(buf, s, k, i):
        for w, (to, zz) in enumerate(((up, plane(-k)), (down, plane(k)))):
            if carried(k, w, i):
                view = buf.at[zz, column(turns[i])]
                send(view, view, az_send.at[s, w, k, i], az_recv.at[s, w, k, i], to)

    def a_wait(buf, s, k, i):
        for w, zz in enumerate((plane(-1 - k), plane(1 + k))):
            if carried(k, w, i):
                arrived(buf.at[zz, column(turns[i])], az_recv.at[s, w, k, i])

    def b_send(buf, s, k):
        for w, (to, zz) in enumerate(((up, plane(-k)), (down, plane(k)))):
            if k < last or w == 0:
                send(buf.at[zz, mine], buf.at[zz, mine], bz_send.at[s, w, k], bz_recv.at[s, w, k], to)

    def b_wait(buf, s, k):
        for w, zz in enumerate((plane(-1 - k), plane(1 + k))):
            if k < last or w == 0:
                arrived(buf.at[zz, mine], bz_recv.at[s, w, k])

    def b_spread(buf, s, offsets):
        for o in offsets:
            for d in range(1, NX):
                there = dev(lax.rem(x + d, NX), z, yl, yh, c)
                view = buf.at[plane(o), mine]
                side = plane(o) // (NZ // 2)
                remote(view, view, bx_send.at[s, d - 1], bx_recv.at[s, d - 1, side], there).start()

    def wait_spread(buf, s, side):
        for d in range(1, NX):
            planes = pl.ds(pl.multiple_of(side * (NZ // 2), NZ // 2), NZ // 2)
            arrived(buf.at[planes, column(NX - d)], bx_recv.at[s, d - 1, side])

    def stream(a_buf, b_buf, s):
        def start():
            a_send(a_buf, s, 0, 0)
            b_send(b_buf, s, 0)
            first_x(a_buf, s)
            b_spread(b_buf, s, (0,))

        def from_x(i):
            arrived(a_buf.at[z, column(turns[i])], ax_recv.at[s, NX - turns[i] - 1])
            a_send(a_buf, s, 0, i)

        def b_step(k):
            b_wait(b_buf, s, k)
            if k < last:
                b_send(b_buf, s, k + 1)
            b_spread(b_buf, s, (-1 - k,) if k == last else (-1 - k, 1 + k))

        def a_step(k, i):
            a_wait(a_buf, s, k, i)
            a_send(a_buf, s, k + 1, i)

        steps = [start]
        steps += [functools.partial(from_x, i) for i in range(1, NX)]
        for k in range(last + 1):
            steps.append(functools.partial(b_step, k))
            if k < last:
                steps += [functools.partial(a_step, k, i) for i in range(NX)]
        return steps

    def last_blocks(a_buf, s):
        for i in range(NX):
            a_wait(a_buf, s, last, i)

    out_steps = stream(oa, ob, 1)

    def pump(count):
        for _ in range(min(count, len(out_steps))):
            out_steps.pop(0)()

    in_steps = stream(wa, wb, 0)
    in_steps.pop(0)()

    away_rows = half * (1 - yl)
    own_rows = half * yl
    for s in range(2):
        src = xs.at[pl.ds(pl.multiple_of(s * rows + away_rows, half), half)]
        send(src, rr.at[yl, pl.ds(s * half, half)], res_send.at[s], res_recv.at[s], partner)
        rr[yl, s * half:(s + 1) * half, :] = xs[pl.ds(pl.multiple_of(s * rows + own_rows, half), half), :]

    def as_column(row):
        grid = (rows, rows)
        diagonal = lax.broadcasted_iota(jnp.int32, grid, 0) == lax.broadcasted_iota(jnp.int32, grid, 1)
        spread = jnp.broadcast_to(row[...].astype(f32), grid)
        return jnp.sum(jnp.where(diagonal, spread, 0.0), axis=1, keepdims=True)

    size = kc.shape[2]
    for number, step in enumerate(in_steps):
        step()
        if number == 1 * len(in_steps) // 2:
            pump(1)

    for k in range(NYH):
        slot = xg.at[k // (NYH // 2), (k % (NYH // 2)) * 2 + c]
        arrived(slot, xs_recv.at[k])
        send(slot, slot, sib_send.at[k], sib_recv.at[k], sib)
    for k in range(NYH):
        arrived(xg.at[k // (NYH // 2), (k % (NYH // 2)) * 2 + (1 - c)], sib_recv.at[k])

    wide[...] = gain[...].astype(f32)
    piece = min(128, width)
    for g in range(2):
        total = jnp.zeros((both, 1), f32)
        for j in range(tile_blocks):
            values = xg[g, j].astype(f32)
            total = total + jnp.sum(values * values, axis=1, keepdims=True)
            for p in range(width // piece):
                row = (yl * tile_blocks + j) * (width // piece) + p
                xn[g, :, j * width + p * piece:j * width + (p + 1) * piece] = (
                    values[:, p * piece:(p + 1) * piece] * wide[pl.ds(row, 1), :]
                ).astype(bf16)
        ssb[g] = jnp.broadcast_to(total, (both, 128))
    send(ssb.at[1 - yl], ssr, pair_send.at[0], pair_recv.at[0], partner)
    pump(2)

    first_at = as_column(pos_ref)
    angle = jnp.concatenate([first_at, first_at + 1.0], axis=0) * freq_ref[...]
    lane = lax.broadcasted_iota(jnp.int32, (both, size), 1)
    cosine = jnp.cos(angle)
    sine = jnp.where(lane < size // 2, -1.0, 1.0) * jnp.sin(angle)
    live_rows = jnp.broadcast_to(as_column(len_ref), (rows, kc.shape[1]))

    for s in range(2):
        arrived(rr.at[1 - yl, pl.ds(s * half, half)], res_recv.at[s])
    order = one_hot_rows((NZ, 2, NX), lambda z_, s_, x_: s_ * half + z_ * NX + x_)
    for g in range(2):
        rr[g] = pick(order, rr[g]).astype(bf16)

    pump(1)
    wait_spread(wb, 0, 0)
    wait_spread(wb, 0, 1)
    depth = NZ * NX * block
    weight_b = wb[...].reshape(depth, wb.shape[2])
    theirs = xn[1 - yl]
    qs[:, cut:] = jnp.dot(theirs, weight_b, preferred_element_type=f32).astype(bf16)
    rest = pl.ds(cut, qs.shape[1] - cut)
    send(qs.at[:, rest], qr.at[:, rest], pair_send.at[3], pair_recv.at[3], partner)
    last_blocks(wa, 0)
    weight_a = wa[...].reshape(depth, cut)
    qs[:, :cut] = jnp.dot(theirs, weight_a, preferred_element_type=f32).astype(bf16)
    send(qs.at[:, 0:cut], qr.at[:, 0:cut], pair_send.at[1], pair_recv.at[1], partner)
    pump(2)
    ours = xn[yl]
    got_a = jnp.dot(ours, weight_a, preferred_element_type=f32)
    got_b = jnp.dot(ours, weight_b, preferred_element_type=f32)
    got = jnp.concatenate([got_a, got_b], axis=1)
    pump(2)
    arrived(ssr, pair_recv.at[0])
    square = (ssb[yl] + ssr[...]) * (1.0 / (2 * tile_blocks * width))
    inverse = lax.rsqrt(square[:, :1] + RMS_EPS)
    arrived(qr.at[:, 0:cut], pair_recv.at[1])
    arrived(qr.at[:, rest], pair_recv.at[3])
    pump(1)
    got = (got + qr[...].astype(f32)) * inverse
    heads = wq.shape[1] // size

    def rotated(v):
        return (v * cosine + pltpu.roll(v, size // 2, 1) * sine).astype(bf16).astype(f32)

    for h in range(heads):
        q = rotated(got[:, h * size:(h + 1) * size])
        for s in range(2):
            q3[:, s * heads + h, :] = q[s * rows:(s + 1) * rows]
    k_new = rotated(got[:, heads * size:(heads + 1) * size])
    v_new = got[:, (heads + 1) * size:(heads + 2) * size].astype(bf16).astype(f32)
    pump(2)

    key_load.wait()
    value_load.wait()
    scale = size ** -0.5
    slots = kc.shape[1]
    lane = lax.broadcasted_iota(jnp.int32, (CHUNK, 2 * heads, slots), 2).astype(f32)
    step_of = lax.broadcasted_iota(jnp.int32, (CHUNK, 2 * heads, 1), 1)
    for r0 in range(0, rows, CHUNK):
        pump(2)
        part = slice(r0, r0 + CHUNK)
        q = q3[part]
        scores = lax.dot_general(
            q.astype(bf16), kc[part], (((2,), (2,)), ((0,), (0,))), preferred_element_type=f32
        ) * scale
        live = live_rows[part][:, None, :]
        scores = jnp.where(lane < live, scores, -jnp.inf)
        k0, k1 = k_new[r0:r0 + CHUNK][:, None, :], k_new[rows + r0:rows + r0 + CHUNK][:, None, :]
        v0, v1 = v_new[r0:r0 + CHUNK][:, None, :], v_new[rows + r0:rows + r0 + CHUNK][:, None, :]
        n0 = jnp.sum(q * k0, axis=2, keepdims=True) * scale
        n1 = jnp.sum(q * k1, axis=2, keepdims=True) * scale
        n1 = jnp.where(step_of >= heads, n1, -jnp.inf)
        top = jnp.maximum(jnp.max(scores, axis=2, keepdims=True), jnp.maximum(n0, n1))
        probs = jnp.exp(scores - top)
        e0, e1 = jnp.exp(n0 - top), jnp.exp(n1 - top)
        total = jnp.sum(probs, axis=2, keepdims=True) + e0 + e1
        mixed = lax.dot_general(
            probs.astype(bf16), vc[part], (((2,), (1,)), ((0,), (0,))), preferred_element_type=f32
        )
        mixed = mixed + e0.astype(bf16).astype(f32) * v0 + e1.astype(bf16).astype(f32) * v1
        att3[part] = mixed / total
        if (r0 + CHUNK) % half == 0:
            lo = r0 + CHUNK - half
            attended = jnp.concatenate(
                [
                    jnp.concatenate([att3[lo:lo + half, s * heads + h, :] for h in range(heads)], axis=1)
                    for s in range(2)
                ],
                axis=0,
            ).astype(bf16)
            attb[yl, 2 * lo:2 * (lo + half), :] = pick(order, attended).astype(bf16)
            group = attb.at[yl, pl.ds(2 * lo, rows)]
            send(group, group, pair_send.at[4 + lo // half], pair_recv.at[4 + lo // half], partner)
    pump(len(out_steps))
    near = z // (NZ // 2)
    wait_spread(ob, 1, near)
    for r in range(2):
        arrived(attb.at[1 - yl, pl.ds(r * rows, rows)], pair_recv.at[4 + r])
    full = attb[...].reshape(2 * both, heads * size)
    tiles = NYH // 2
    slab = NZ // tile_blocks

    def project(j):
        left = oa[pl.ds(j * slab, slab)].reshape(width, ocut)
        right = ob[pl.ds(j * slab, slab)].reshape(width, ob.shape[2])
        dims = (((1,), (1,)), ((), ()))
        return lax.dot_general(
            full[:, :ocut], left, dims, preferred_element_type=f32
        ) + lax.dot_general(full[:, ocut:], right, dims, preferred_element_type=f32)

    def at(yy):
        yy = lax.rem(yy + ny, ny)
        return dev(x, z, lax.rem(yy, 2), yy // 2, c)

    def ahead(m):
        return lax.rem(NYH * yl + m - y + 2 * ny, ny)

    cuts = [pl.ds(0, split), pl.ds(split, width - split)]

    def either(delta, *values):
        hit = delta == values[0]
        for value in values[1:]:
            hit = jnp.logical_or(hit, delta == value)
        return hit

    def far_copy(m, h, to):
        return remote(sp.at[m, :, cuts[h]], fb.at[m, :, cuts[h]], y_send.at[m, h], f_recv.at[m, h], to)

    def near_copy(m, h, side, to):
        return remote(sp.at[m, :, cuts[h]], rb.at[side, :, cuts[h]], y_send.at[m, h], y_recv.at[side, h], to)

    half_tiles = (near, 1 - near)
    for n, i in enumerate(half_tiles):
        if n == 1:
            last_blocks(oa, 1)
            wait_spread(ob, 1, i)
        ps[i] = project(2 * i + 1 - c).astype(bf16)
        send(ps.at[i], pr.at[i], core_send.at[i], core_recv.at[i], sib)
        kept = project(2 * i + c)
        arrived(pr.at[i], core_recv.at[i])
        summed = (kept + pr[i].astype(f32)).astype(bf16)
        for r in range(2):
            for g in range(2):
                lo = g * both + r * rows
                sp[2 * i + r, g * rows:(g + 1) * rows, :] = summed[lo:lo + rows]
        for h in range(2):
            for m in (2 * i, 2 * i + 1):
                delta = ahead(m)
                pl.when(either(delta, 3, 4) if h == 0 else delta == 3)(far_copy(m, h, at(y + 2)).start)
                pl.when(delta == 5 if h == 0 else either(delta, 4, 5))(far_copy(m, h, at(y - 2)).start)
                if h == 0:
                    pl.when(delta == 6)(near_copy(m, h, 1, at(NYH * yl + m)).start)
                else:
                    pl.when(delta == 2)(near_copy(m, h, 0, at(NYH * yl + m)).start)
    for h in range(2):
        lanes = slice(0, split) if h == 0 else slice(split, width)
        for m in [2 * i + r for i in half_tiles for r in range(2)]:
            delta = ahead(m)

            @pl.when(either(delta, 1, 7, 2 if h == 0 else 6))
            def _():
                arrived(fb.at[m, :, cuts[h]], f_recv.at[m, h])
                sp[m, :, lanes] = (sp[m, :, lanes].astype(f32) + fb[m, :, lanes].astype(f32)).astype(bf16)

            pl.when(either(delta, 1, 2) if h == 0 else delta == 1)(near_copy(m, h, 0, at(NYH * yl + m)).start)
            pl.when(delta == 7 if h == 0 else either(delta, 6, 7))(near_copy(m, h, 1, at(NYH * yl + m)).start)

    holds = jnp.where(y // NYH == yl, 1.0, 0.0)
    for h in range(2):
        lanes = slice(0, split) if h == 0 else slice(split, width)
        result = rr[:, :, lanes].reshape(both, -1).astype(f32)
        result = result + sp[lax.rem(y, NYH), :, lanes].astype(f32) * holds
        for side in range(2):
            arrived(rb.at[side, :, cuts[h]], y_recv.at[side, h])
            result = result + rb[side, :, lanes].astype(f32)
        result = result.reshape(2, NZ, 2 * NX, result.shape[1])
        for k in range(NZ):
            zs[k, :, lanes] = jnp.concatenate([result[0, k], result[1, k]], axis=0).astype(bf16)
        zr[z, :, lanes] = zs[z, :, lanes]
        for d in range(1, NZ):
            zz = lax.rem(z + d, NZ)
            send(zs.at[zz, :, cuts[h]], zr.at[z, :, cuts[h]], za_send.at[h, d - 1], za_recv.at[h, d - 1],
                 dev(x, zz, yl, yh, c))
    order = one_hot_rows(
        (NX, 2, NZ, 2), lambda x_, g_, z_, s_: ((z_ * 2 + g_) * 2 + s_) * NX + x_
    )
    for h in range(2):
        lanes = slice(0, split) if h == 0 else slice(split, width)
        for d in range(1, NZ):
            arrived(zr.at[lax.rem(z + NZ - d, NZ), :, cuts[h]], za_recv.at[h, d - 1])
        moved = pick(order, zr[:, :, lanes].reshape(both, -1)).astype(bf16)
        xo[:, :, lanes] = moved.reshape(NX, 4 * NZ, moved.shape[1])
        xr[x, :, lanes] = xo[x, :, lanes]
        for d in range(1, NX):
            xx = lax.rem(x + d, NX)
            send(xo.at[xx, :, cuts[h]], xr.at[x, :, cuts[h]], xa_send.at[h, d - 1], xa_recv.at[h, d - 1],
                 dev(xx, z, yl, yh, c))
    order = one_hot_rows(
        (2, NZ, NX, 2), lambda g_, z_, x_, s_: ((x_ * 2 + g_) * NZ + z_) * 2 + s_
    )
    for h in range(2):
        lanes = slice(0, split) if h == 0 else slice(split, width)
        for d in range(1, NX):
            arrived(xr.at[lax.rem(x + NX - d, NX), :, cuts[h]], xa_recv.at[h, d - 1])
        out[:, lanes] = pick(order, xr[:, :, lanes].reshape(both, -1)).astype(bf16)

    for copy in sent:
        copy.wait_send()
    for s, buf in ((0, wb), (1, ob)):
        for d in range(1, NX):
            view = buf.at[:, mine]
            remote(view, view, bx_send.at[s, d - 1], bx_recv.at[s, d - 1, 0], sib).wait_send()
    for k in range(NYH):
        is_self = jnp.logical_and(yl_to == yl, yh == k)
        away = remote(xs, xg.at[yl, tile_me], xs_send.at[k], xs_recv.at[src_me], sib)
        pl.when(jnp.logical_not(is_self))(away.wait_send)
        for h in range(2):
            pl.when(ahead(k) != 0)(far_copy(k, h, sib).wait_send)


def on_device(
    hidden, next_hidden, gain, w_query, w_key, w_value, w_out,
    key_cache, value_cache, lengths, positions,
):
    rows, width = hidden.shape
    both = 2 * rows
    slots, size = key_cache.shape[2], key_cache.shape[3]
    block, qcols = w_query.shape
    heads = qcols // size
    columns = qcols + 2 * size
    cut, ocut = columns // 2, qcols // 2
    half_width = NYH * width

    tall = gain.reshape(-1, min(128, width))
    place = np.arange(size) % (size // 2)
    freqs = (ROPE_BASE ** (-(2.0 * place) / size)).astype(np.float32)[None, :]

    vmem = pl.BlockSpec(memory_space=pltpu.VMEM)
    hbm = pl.BlockSpec(memory_space=pl.ANY)
    dma = lambda *shape: pltpu.SemaphoreType.DMA(shape)
    steps = NZ // 2
    result = pl.pallas_call(
        layer_kernel,
        out_shape=jax.ShapeDtypeStruct((both, width), bf16),
        in_specs=[vmem] * 10 + [hbm] * 2,
        out_specs=vmem,
        scratch_shapes=[
            pltpu.VMEM((NZ, NX * block, cut), bf16),
            pltpu.VMEM((NZ, NX * block, columns - cut), bf16),
            pltpu.VMEM((NZ, NX * block, ocut), bf16),
            pltpu.VMEM((NZ, NX * block, qcols - ocut), bf16),
            pltpu.VMEM((both, width), bf16),
            pltpu.VMEM((2, NYH, both, width), bf16),
            pltpu.VMEM((2, both, half_width), bf16),
            pltpu.VMEM(tall.shape, f32),
            pltpu.VMEM((2, both, 128), f32),
            pltpu.VMEM((both, 128), f32),
            pltpu.VMEM((both, columns), bf16),
            pltpu.VMEM((both, columns), bf16),
            pltpu.VMEM((rows, slots, size), bf16),
            pltpu.VMEM((rows, slots, size), bf16),
            pltpu.VMEM((rows, 2 * heads, size), f32),
            pltpu.VMEM((rows, 2 * heads, size), f32),
            pltpu.VMEM((2, both, qcols), bf16),
            pltpu.VMEM((NYH // 2, 2 * both, width), bf16),
            pltpu.VMEM((NYH // 2, 2 * both, width), bf16),
            pltpu.VMEM((NYH, both, width), bf16),
            pltpu.VMEM((NYH, both, width), bf16),
            pltpu.VMEM((2, both, width), bf16),
            pltpu.VMEM((2, rows, width), bf16),
            pltpu.VMEM((NZ, 4 * NX, width), bf16),
            pltpu.VMEM((NZ, 4 * NX, width), bf16),
            pltpu.VMEM((NX, 4 * NZ, width), bf16),
            pltpu.VMEM((NX, 4 * NZ, width), bf16),
            dma(2),
            dma(NYH), dma(NYH), dma(NYH), dma(NYH), dma(2), dma(2),
            dma(2, NX - 1), dma(2, NX - 1), dma(2, 2, steps, NX), dma(2, 2, steps, NX),
            dma(2, NX - 1), dma(2, NX - 1, 2), dma(2, 2, steps), dma(2, 2, steps),
            dma(6), dma(6), dma(NYH // 2), dma(NYH // 2), dma(NYH, 2), dma(NYH, 2), dma(2, 2),
            dma(2, NZ - 1), dma(2, NZ - 1), dma(2, NX - 1), dma(2, NX - 1),
        ],
        compiler_params=pltpu.CompilerParams(
            collective_id=0, has_side_effects=True, vmem_limit_bytes=56 * 1024 * 1024
        ),
        name="gathered_layer",
    )(
        hidden, next_hidden, tall, w_query, w_key, w_value, w_out.T,
        jnp.asarray(freqs), lengths[None, :], positions[None, :],
        key_cache.reshape(rows, slots, size), value_cache.reshape(rows, slots, size),
    )
    return result.reshape(rows, 2, 1, width)


def solution(mesh):
    placed = (
        P("fsdp", "tp"),
        P("fsdp", "tp"),
        P(),
        P("fsdp", "tp"),
        P("fsdp", "tp"),
        P("fsdp", "tp"),
        P("tp", "fsdp"),
        P("fsdp", "tp", None, None),
        P("fsdp", "tp", None, None),
        P("fsdp"),
        P("fsdp"),
    )
    return jax.shard_map(
        on_device,
        mesh=mesh,
        in_specs=placed,
        out_specs=P(None, None, "fsdp", "tp"),
        check_vma=False,
    )
```
